128 devices in a mesh: dom: 32 (over x, z, core), sub: 4 (over y).
Axes of the slice: x: 4, y: 4, z: 4, core: 2. Of those that a mesh axis runs over, the one named last changes fastest.
Arguments:
- dofs: float32 [9, 20, 65536], P(None, None, ('dom', 'sub')), may hold values from -6 to 6
- star: float32 [3, 9, 9, 65536], P(None, None, None, ('dom', 'sub')), may hold values from -1.25 to 1.25
- stiff: float32 [3, 20, 20], replicated, may hold values from -1.25 to 1.25
- flux_local: float32 [4, 20, 20], replicated, may hold values from -1.25 to 1.25
- flux_neighbor: float32 [4, 12, 20, 20], replicated, may hold values from -1.25 to 1.25
- solver_minus: float32 [4, 9, 9, 65536], P(None, None, None, ('dom', 'sub')), may hold values from -1 to 1
- solver_plus: float32 [4, 9, 9, 65536], P(None, None, None, ('dom', 'sub')), may hold values from -1 to 1
- neighbor: int32 [4, 65536], P(None, ('dom', 'sub')), may hold values from 0 to 767
- orientation: int32 [4, 65536], P(None, ('dom', 'sub')), may hold values from 0 to 11
- copy_list: int32 [2, 16384], P(None, ('dom', 'sub')), may hold values from 0 to 511
- face_lift: float32 [4, 10, 20], replicated, may hold values from -1.25 to 1.25
- face_eval: float32 [25, 10], replicated, may hold values from -2 to 2
- face_weight: float32 [10, 25], replicated, may hold values from -1.25 to 1.25
- side_owner: int32 [65536, 2], P(('dom', 'sub')), may hold values from 0 to 127, as said below
- side_face: int32 [65536, 2], P(('dom', 'sub')), may hold values from 0 to 2047
- impedance: float32 [4, 65536], P(None, ('dom', 'sub')), may hold values from 0.5 to 2
- normal_initial: float32 [25, 65536], P(None, ('dom', 'sub')), may hold values from -3 to -1
- shear_initial: float32 [2, 25, 65536], P(None, None, ('dom', 'sub')), may hold values from -6 to 6
- slip: float32 [25, 65536], P(None, ('dom', 'sub')), may hold values from 0 to 1
- static_friction: float32 [25, 65536], P(None, ('dom', 'sub')), may hold values from 0.5 to 0.8
- friction_drop: float32 [25, 65536], P(None, ('dom', 'sub')), may hold values from 0.1 to 0.4
- slip_scale: float32 [25, 65536], P(None, ('dom', 'sub')), may hold values from 0.2 to 0.8
Outputs:
- new_dofs: float32 [9, 20, 65536], P(None, None, ('dom', 'sub'))
- new_slip: float32 [25, 65536], P(None, ('dom', 'sub'))
- traction: float32 [2, 25, 65536], P(None, None, ('dom', 'sub'))
The draws below stay inside these ranges and needn't reach their ends.
Inputs may be any that keep to these rules, and one draw needn't show every extreme that they name: `side_owner`: the two sides of a fault face lie on devices whose indices differ by one; among the 512 faces of one device, no device holds more than 24 sides, and in every such block some device holds exactly 24.
All inputs are finite; a program needn't handle non-finite values.
Results may differ from the reference program's by a relative error of at most 0.0001.
Values sent between devices are 32-bit elements; how exact they have to be, the bound alone decides.
No kernel may reach another device: no remote copies, remote signals or barrier semaphores. Data moves between devices by JAX's collectives and lax.ppermute only.
A program may use at most 256 MiB of HBM per device.

```python
import math
import jax
import jax.numpy as jnp
from jax import lax

NB = 20
NQ = 9
NG = 25
NFM = 10
NCOMB = 12
E_DEV = 512
F_DEV = 512
H = 128
NDEV = 128
CAP = 24
ELEMS = 65536
FAULTS = 65536


def draw_side_owner(key, part):
    key = jax.random.fold_in(key, 11)
    keys = jax.random.split(key, NDEV)

    def one_block(block_key):
        first_key, second_key, third_key = jax.random.split(block_key, 3)
        order = jax.random.permutation(first_key, NDEV // 2)
        pairs = order[jnp.arange(F_DEV, dtype=jnp.int32) // CAP]
        pairs = pairs[jax.random.permutation(second_key, F_DEV)]
        flipped = jax.random.randint(third_key, (F_DEV,), 0, 2)
        lowest = 2 * pairs
        return jnp.stack([lowest + flipped, lowest + 1 - flipped], axis=1)
    return jax.vmap(one_block)(keys).reshape(FAULTS, 2).astype(jnp.int32)


def place_ends(entries, stream_key, low, largest):
    shape = entries.shape
    spot = [jax.random.randint(jax.random.fold_in(stream_key, axis), (), 0, shape[axis]) for axis in range(len(shape))]
    entries = entries.at[tuple(spot)].set(low)
    longest = shape.index(max(shape))
    spot[longest] = (spot[longest] + 1) % shape[longest]
    return entries.at[tuple(spot)].set(largest)


def block_levels(stream_key, extent, cuts, least, largest):
    def one(position, shards_of):
        draws = jax.random.uniform(jax.random.fold_in(jax.random.fold_in(stream_key, 6), position), (shards_of,), jnp.float32, least / len(cuts), largest / len(cuts))
        return jnp.repeat(jnp.exp(draws), extent[position] // shards_of).reshape((-1,) + (1,) * (len(extent) - position - 1))

    gain = one(*cuts[0])
    for cut in cuts[1:]:
        gain = gain * one(*cut)
    return gain


def bell_draw(stream_key, shape, width, reach, shards=(), held_as=jnp.bfloat16):
    values = width * jax.random.normal(stream_key, shape, jnp.float32)
    if shards:
        values = values * block_levels(stream_key, shape, shards, -0.22, 0.18)
    return jnp.clip(values, -reach, reach).astype(held_as)


def setup_inputs(seed: int = 0) -> dict:
    streams_of = jax.random.split(jax.random.key(seed), 23)
    return {
        "dofs": bell_draw(streams_of[0], (NQ, NB, ELEMS), 1.0, 6.0, ((2, 128),), jnp.float32),
        "star": bell_draw(streams_of[1], (3, NQ, NQ, ELEMS), (3 * NQ) ** -0.5, 1.25, ((3, 128),), jnp.float32),
        "stiff": bell_draw(streams_of[2], (3, NB, NB), NB ** -0.5, 1.25, (), jnp.float32),
        "flux_local": bell_draw(streams_of[3], (4, NB, NB), NB ** -0.5, 1.25, (), jnp.float32),
        "flux_neighbor": bell_draw(streams_of[4], (4, NCOMB, NB, NB), NB ** -0.5, 1.25, (), jnp.float32),
        "solver_minus": bell_draw(streams_of[5], (4, NQ, NQ, ELEMS), (4 * NQ) ** -0.5, 1.0, ((3, 128),), jnp.float32),
        "solver_plus": bell_draw(streams_of[6], (4, NQ, NQ, ELEMS), (4 * NQ) ** -0.5, 1.0, ((3, 128),), jnp.float32),
        "neighbor": place_ends(jax.random.randint(streams_of[7], (4, ELEMS), 0, E_DEV + 2 * H), jax.random.fold_in(streams_of[7], 1), 0, (E_DEV + 2 * H) - 1).astype(jnp.int32),
        "orientation": place_ends(jax.random.randint(streams_of[8], (4, ELEMS), 0, NCOMB), jax.random.fold_in(streams_of[8], 1), 0, NCOMB - 1).astype(jnp.int32),
        "copy_list": place_ends(jax.random.randint(streams_of[9], (2, NDEV * H), 0, E_DEV), jax.random.fold_in(streams_of[9], 1), 0, E_DEV - 1).astype(jnp.int32),
        "face_lift": bell_draw(streams_of[10], (4, NFM, NB), NB ** -0.5, 1.25, (), jnp.float32),
        "face_eval": bell_draw(streams_of[11], (NG, NFM), NFM ** -0.5, 2.0, (), jnp.float32),
        "face_weight": bell_draw(streams_of[12], (NFM, NG), NG ** -0.5, 1.25, (), jnp.float32),
        "side_owner": draw_side_owner(jax.random.fold_in(streams_of[22], 71), 0),
        "side_face": place_ends(jax.random.randint(streams_of[14], (FAULTS, 2), 0, 4 * E_DEV), jax.random.fold_in(streams_of[14], 1), 0, (4 * E_DEV) - 1).astype(jnp.int32),
        "impedance": jnp.clip(jnp.exp(math.log(2.0) - 1.3862944 * jax.random.uniform(streams_of[15], (4, FAULTS), jnp.float32) ** block_levels(streams_of[15], (4, FAULTS), ((1, 128),), -0.2, 0.2)), 0.5, 2.0),
        "normal_initial": jnp.clip(-3.0 + 2.0 * jax.random.uniform(streams_of[16], (NG, FAULTS), jnp.float32) ** block_levels(streams_of[16], (NG, FAULTS), ((1, 128),), -0.2, 0.2), -3.0, -1.0),
        "shear_initial": bell_draw(streams_of[17], (2, NG, FAULTS), 1.0, 6.0, ((2, 128),), jnp.float32),
        "slip": jnp.clip(1.0 * jax.random.uniform(streams_of[18], (NG, FAULTS), jnp.float32) ** block_levels(streams_of[18], (NG, FAULTS), ((1, 128),), -0.2, 0.2), 0.0, 1.0),
        "static_friction": jnp.clip(0.5 + 0.3 * jax.random.uniform(streams_of[19], (NG, FAULTS), jnp.float32) ** block_levels(streams_of[19], (NG, FAULTS), ((1, 128),), -0.2, 0.2), 0.5, 0.8),
        "friction_drop": jnp.clip(0.1 + 0.3 * jax.random.uniform(streams_of[20], (NG, FAULTS), jnp.float32) ** block_levels(streams_of[20], (NG, FAULTS), ((1, 128),), -0.2, 0.2), 0.1, 0.4),
        "slip_scale": jnp.clip(jnp.exp(math.log(0.8) - 1.3862944 * jax.random.uniform(streams_of[21], (NG, FAULTS), jnp.float32) ** block_levels(streams_of[21], (NG, FAULTS), ((1, 128),), -0.2, 0.2)), 0.2, 0.8),
    }


time_step = 0.8
trace_rows = (0, 3, 5, 6, 7, 8)

def predictor(dofs, star, stiff):
    highest = lax.Precision.HIGHEST
    current = dofs
    integral = time_step * dofs
    factor = time_step
    for order in range(1, 4):
        moved = jnp.einsum('dbc,qce->dqbe', stiff, current, precision=highest)
        current = -jnp.einsum('dqpe,dqbe->pbe', star, moved, precision=highest)
        factor = factor * time_step / (order + 1)
        integral = integral + factor * current
    return integral

def friction(minus, plus, impedance, normal_initial, shear_initial, slip, static_friction, friction_drop, slip_scale):
    pwave_minus = impedance[0][None, :]
    pwave_plus = impedance[1][None, :]
    swave_minus = impedance[2][None, :]
    swave_plus = impedance[3][None, :]
    normal = (pwave_plus * minus[0] + pwave_minus * plus[0] + pwave_minus * pwave_plus * (plus[3] - minus[3])) / (pwave_minus + pwave_plus)
    swave_sum = swave_minus + swave_plus
    viscous = swave_minus * swave_plus / swave_sum
    shear = (swave_plus * minus[1:3] + swave_minus * plus[1:3] + swave_minus * swave_plus * (plus[4:6] - minus[4:6])) / swave_sum + shear_initial
    weakened = jnp.minimum(slip / slip_scale, 1.0)
    coefficient = static_friction - friction_drop * weakened
    strength = coefficient * jnp.maximum(-(normal + normal_initial), 0.0)
    magnitude = jnp.sqrt(shear[0] * shear[0] + shear[1] * shear[1])
    ratio = jnp.minimum(1.0, strength / jnp.maximum(magnitude, 1.0))
    final = shear * ratio
    rates = (shear - final) / viscous
    new_slip = slip + time_step * jnp.sqrt(rates[0] * rates[0] + rates[1] * rates[1])
    imposed = final - shear_initial
    jump_minus = normal - minus[0]
    jump_plus = normal - plus[0]
    delta_minus = jnp.stack([jump_minus, imposed[0] - minus[1], imposed[1] - minus[2], jump_minus / pwave_minus, (imposed[0] - minus[1]) / swave_minus, (imposed[1] - minus[2]) / swave_minus])
    delta_plus = jnp.stack([jump_plus, imposed[0] - plus[1], imposed[1] - plus[2], -jump_plus / pwave_plus, -(imposed[0] - plus[1]) / swave_plus, -(imposed[1] - plus[2]) / swave_plus])
    return (new_slip, final, delta_minus, delta_plus)

def neighbor_ids(neighbor, copy_list):
    device = (jnp.arange(ELEMS, dtype=jnp.int32) // E_DEV)[None, :]
    lower_slot = jnp.clip(neighbor - E_DEV, 0, H - 1)
    upper_slot = jnp.clip(neighbor - E_DEV - H, 0, H - 1)
    lower_dev = jnp.clip(device - 1, 0, NDEV - 1)
    upper_dev = jnp.clip(device + 1, 0, NDEV - 1)
    lower_elem = copy_list[1][lower_dev * H + lower_slot]
    upper_elem = copy_list[0][upper_dev * H + upper_slot]
    own = neighbor < E_DEV
    is_lower = jnp.logical_and(neighbor >= E_DEV, neighbor < E_DEV + H)
    global_id = jnp.where(own, device * E_DEV + neighbor, jnp.where(is_lower, lower_dev * E_DEV + lower_elem, upper_dev * E_DEV + upper_elem))
    valid = own | is_lower & (device > 0) | ~own & ~is_lower & (device < NDEV - 1)
    return (global_id.astype(jnp.int32), valid)

def reference(dofs, star, stiff, flux_local, flux_neighbor, solver_minus, solver_plus, neighbor, orientation, copy_list, face_lift, face_eval, face_weight, side_owner, side_face, impedance, normal_initial, shear_initial, slip, static_friction, friction_drop, slip_scale):
    highest = lax.Precision.HIGHEST
    integral = predictor(dofs, star, stiff)
    moved = jnp.einsum('dcb,qce->dqbe', stiff, integral, precision=highest)
    volume = jnp.einsum('dqpe,dqbe->pbe', star, moved, precision=highest)
    local = jnp.zeros_like(dofs)
    neighbour = jnp.zeros_like(dofs)
    global_id, valid = neighbor_ids(neighbor, copy_list)
    for face in range(4):
        projected = jnp.einsum('bc,qce->qbe', flux_local[face], integral, precision=highest)
        local = local + jnp.einsum('qpe,qbe->pbe', solver_minus[face], projected, precision=highest)
        gathered = integral[:, :, global_id[face]] * valid[face].astype(jnp.float32)[None, None, :]
        chosen = flux_neighbor[face][orientation[face]]
        projected = jnp.einsum('ebc,qce->qbe', chosen, gathered, precision=highest)
        neighbour = neighbour + jnp.einsum('qpe,qbe->pbe', solver_plus[face], projected, precision=highest)
    rows = jnp.array(trace_rows, dtype=jnp.int32)
    flat_face = side_face.reshape(-1)
    element = side_owner.reshape(-1) * E_DEV + flat_face % E_DEV
    face_index = flat_face // E_DEV
    columns = integral[rows][:, :, element]
    lifts = face_lift[face_index]
    modal = jnp.einsum('nmc,kcn->kmn', lifts, columns, precision=highest)
    trace = jnp.einsum('gm,kmn->kgn', face_eval, modal, precision=highest) / time_step
    trace = trace.reshape(6, NG, FAULTS, 2)
    new_slip, traction, delta_minus, delta_plus = friction(trace[..., 0], trace[..., 1], impedance, normal_initial, shear_initial, slip, static_friction, friction_drop, slip_scale)
    delta = jnp.stack([delta_minus, delta_plus], axis=-1).reshape(6, NG, 2 * FAULTS)
    projected = jnp.einsum('mg,kgn->kmn', face_weight, delta, precision=highest)
    contrib = jnp.einsum('nmc,kmn->kcn', lifts, projected, precision=highest)
    fault_sum = jnp.zeros((6, NB, ELEMS), jnp.float32).at[:, :, element].add(contrib)
    fault = jnp.zeros_like(dofs).at[rows].set(fault_sum)
    new_dofs = dofs + volume - local - neighbour + fault
    return (new_dofs, new_slip, traction)
```

```python
import jax
import jax.numpy as jnp
from jax import lax
from jax.experimental import pallas as pl
from jax.experimental.pallas import tpu as pltpu
from jax.sharding import PartitionSpec as P

time_step = 0.8
trace_rows = (0, 3, 5, 6, 7, 8)
both = ("dom", "sub")
f32 = jnp.float32
bf16 = jnp.bfloat16
vmem = pl.BlockSpec(memory_space=pltpu.VMEM)


def from_behind(block, axis, distance):
    devices = range(lax.axis_size(axis))
    route = [(i - distance, i) for i in devices if i - distance in devices]
    return lax.ppermute(block, axis, route)


def iota(shape, axis):
    return lax.broadcasted_iota(jnp.int32, shape, axis)


def product(a, b, left=1, right=0):
    return lax.dot_general(a, b, (((left,), (right,)), ((), ())), preferred_element_type=f32)


def product_full(a, b, left=1, right=0):
    return lax.dot_general(
        a,
        b,
        (((left,), (right,)), ((), ())),
        precision=lax.Precision.HIGHEST,
        preferred_element_type=f32,
    )


def halves(x):
    high = x.astype(bf16)
    low = (x - high.astype(f32)).astype(bf16)
    return high, low


def flags(condition):
    return jnp.where(condition, 1.0, 0.0).astype(f32)


def pack_left(a):
    repeat = flags((iota((128, 128), 1) & 31) == iota((128, 128), 0))
    wide = product_full(a, repeat)
    high = wide.astype(bf16).astype(f32)
    return jnp.where(iota(wide.shape, 1) < 64, high, wide - high).astype(bf16)


def pack_right(x):
    high, low = halves(x)
    return jnp.concatenate([high, low, high, low], axis=0)


def thirds(t):
    return jnp.where(t >= 10, 1, 0) + jnp.where(t >= 20, 1, 0)


def owner_flags(owner_ref):
    owner = jnp.concatenate([owner_ref[0:1, :], owner_ref[1:2, :]], axis=1)
    return flags(iota((128, owner.shape[1]), 0) == owner)


def request_kernel(owner_ref, face_ref, impedance_ref, request_ref, position_ref):
    owned = owner_flags(owner_ref)
    owned_half = owned.astype(bf16)
    sides = owned.shape[1]
    block = 256
    ahead = flags(iota((block, block), 0) < iota((block, block), 1)).astype(bf16)
    carry = jnp.zeros((128, 1), f32)
    positions = []
    for start in range(0, sides, block):
        part = owned[:, start : start + block]
        before = product(owned_half[:, start : start + block], ahead) + carry
        positions.append(jnp.sum(part * before, axis=0, keepdims=True))
        carry = carry + jnp.sum(part, axis=1, keepdims=True)
    position = jnp.concatenate(positions, axis=1)
    position_ref[...] = jnp.broadcast_to(position, position_ref.shape)
    wanted = jnp.concatenate([face_ref[0:1, :], face_ref[1:2, :]], axis=1).astype(f32) + 1.0
    zp = jnp.concatenate([impedance_ref[0:1, :], -impedance_ref[1:2, :]], axis=1)
    zs = jnp.concatenate([impedance_ref[2:3, :], -impedance_ref[3:4, :]], axis=1)
    row = iota((128, sides), 0)
    channel = jnp.where(row >= 24, 1, 0) + jnp.where(row >= 48, 1, 0)
    slot = (row - 24 * channel).astype(f32)
    value = jnp.where(row < 24, wanted, jnp.where(row < 48, zp, zs))
    value = jnp.where((slot == position) & (row < 72), value, 0.0)
    high = value.astype(bf16)
    rest = value - high.astype(f32)
    middle, low = halves(rest)
    request_ref[...] = (
        product(owned_half, high, 1, 1)
        + product(owned_half, middle, 1, 1)
        + product(owned_half, low, 1, 1)
    )


def lift_expand(lift_ref, lift_pad):
    lift_pad[...] = jnp.zeros_like(lift_pad)
    for face in range(4):
        lift_pad[face * 16 : face * 16 + 10, 0:20] = lift_ref[:, face, :]
    row = iota((256, 64), 0)
    inner = row & 31
    third = thirds(inner)
    source = (row >> 6) * 16 + inner - 10 * third
    pick = flags((source == iota((256, 64), 1)) & (inner < 30))
    rows = product_full(pick, lift_pad[...])
    spread = flags((iota((128, 192), 1) & 31) == iota((128, 192), 0))
    wide = product_full(rows, spread)
    row = iota((256, 192), 0)
    want = ((row >> 5) & 1) * 3 + thirds(row & 31)
    return jnp.where((iota((256, 192), 1) >> 5) == want, wide, 0.0)


def predictor_kernel(
    dofs_ref,
    star_ref,
    stiff_ref,
    lift_ref,
    copy_ref,
    integral_ref,
    modal_ref,
    table_ref,
    lift_out_ref,
    low_ref,
    up_ref,
    current,
    moved,
    left,
    lift_pad,
):
    count = dofs_ref.shape[2]
    left[...] = jnp.zeros_like(left)
    for d in range(3):
        left[d * 32 : d * 32 + 20, 0:20] = stiff_ref[d]
    packed = pack_left(left[...])
    current[...] = jnp.zeros_like(current)
    for q in range(9):
        current[q, 0:20, :] = dofs_ref[q]
        integral_ref[q, :, :] = time_step * current[q, 0:24, :]
    factor = time_step
    for order in range(1, 4):
        factor = factor * time_step / (order + 1)
        for q in range(9):
            moved[q] = product(packed, pack_right(current[q]))

        def tile(i, carry):
            lanes = pl.ds(pl.multiple_of(i * 128, 128), 128)
            total = [jnp.zeros((24, 128), f32) for _ in range(9)]
            for q in range(9):
                for d in range(3):
                    part = moved[q, d * 32 : d * 32 + 24, lanes]
                    for p in range(9):
                        total[p] = total[p] - star_ref[q, p, d : d + 1, lanes] * part
            for p in range(9):
                current[p, 0:24, lanes] = total[p]
                integral_ref[p, :, lanes] += factor * total[p]
            return carry

        lax.fori_loop(0, count // 128, tile, 0)
    whole = integral_ref[...].reshape(216, count)
    high, low = halves(whole)
    for index, out in ((0, low_ref), (1, up_ref)):
        pick = flags(iota((count, 128), 0) == copy_ref[index : index + 1, :]).astype(bf16)
        out[...] = product(high, pick) + product(low, pick)
    spread = lift_expand(lift_ref, lift_pad)
    lift_out_ref[...] = spread
    for p in range(9):
        current[p, 0:24, :] = integral_ref[p]
    rows = jnp.concatenate([current[r] for r in trace_rows], axis=0)
    rows_high, rows_low = halves(rows)
    spread_high, spread_low = halves(spread)
    modal = (
        product(spread_high, rows_high)
        + product(spread_high, rows_low)
        + product(spread_low, rows_high)
    )
    modal_ref[...] = modal
    table_ref[...] = modal.T


def slots_of(request):
    wanted = (request + 0.5).astype(jnp.int32) - 1
    element = jnp.where(wanted < 0, -1, wanted & 511)
    return element, wanted >> 9


def slot_flags(element, first, many, count):
    lane = iota((128, count), 1)
    return jnp.concatenate(
        [
            flags(element[:, k : k + 1] == lane).astype(bf16)
            for k in range(first, first + many)
        ],
        axis=0,
    )


def gather_kernel(request_ref, table_ref, out_ref):
    request = request_ref[...]
    element, face = slots_of(request)
    table = jnp.concatenate(halves(table_ref[...]), axis=1)
    lane = iota((128, 128), 1)
    for r in range(6):
        pick = slot_flags(element, 4 * r, 4, table_ref.shape[0])
        both_halves = product(pick, table)
        found = both_halves[:, 0:256] + both_halves[:, 256:512]
        block = jnp.zeros((128, 128), f32)
        for j in range(4):
            k = 4 * r + j
            mine = found[j * 128 : j * 128 + 128]
            side = face[:, k : k + 1]
            mine = jnp.where(side >= 2, mine[:, 128:256], mine[:, 0:128])
            mine = jnp.where((side & 1) == 1, pltpu.roll(mine, 64, 1), mine)
            velocity = pltpu.roll(mine, 96, 1)
            z = jnp.where(lane < 10, request[:, 24 + k : 25 + k], request[:, 48 + k : 49 + k])
            wave = jnp.where(lane < 32, mine - z * velocity, 0.0)
            if j:
                wave = pltpu.roll(wave, 32 * j, 1)
            block = block + wave
        out_ref[pl.ds(r, 128, stride=8), :] = block
    for r in range(6, 8):
        out_ref[pl.ds(r, 128, stride=8), :] = jnp.zeros((128, 128), f32)


def inner_kernel(integral_ref, star_ref, minus_ref, stiff_ref, local_ref, out_ref, left, square, moved):
    count = integral_ref.shape[2]
    left[...] = jnp.zeros_like(left)
    square[...] = jnp.zeros_like(square)
    for d in range(3):
        square[0:20, 0:20] = stiff_ref[d]
        left[d * 32 : d * 32 + 32, :] = square[...].T[0:32, :]
    for f in range(4):
        left[96 + f * 32 : 96 + f * 32 + 20, 0:20] = local_ref[:, f, :]
    packed = pack_left(left[...])
    empty = jnp.zeros((8, count), f32)
    for q in range(9):
        moved[q] = product(
            packed, pack_right(jnp.concatenate([integral_ref[q], empty], axis=0))
        )

    def tile(i, carry):
        lanes = pl.ds(pl.multiple_of(i * 128, 128), 128)
        total = [jnp.zeros((24, 128), f32) for _ in range(9)]
        for q in range(9):
            for d in range(3):
                part = moved[q, d * 32 : d * 32 + 24, lanes]
                for p in range(9):
                    total[p] = total[p] + star_ref[q, p, d : d + 1, lanes] * part
            for f in range(4):
                part = moved[q, 96 + f * 32 : 96 + f * 32 + 24, lanes]
                for p in range(9):
                    total[p] = total[p] - minus_ref[q, p, f : f + 1, lanes] * part
        for p in range(9):
            out_ref[p, :, lanes] = total[p]
        return carry

    lax.fori_loop(0, count // 128, tile, 0)


def neighbour_kernel(
    inner_ref,
    integral_ref,
    lower_ref,
    upper_ref,
    neighbor_ref,
    orientation_ref,
    plus_ref,
    flux_ref,
    out_ref,
    left,
    moved,
):
    count = integral_ref.shape[2]
    extended = jnp.concatenate(
        [integral_ref[...].reshape(216, count), lower_ref[...], upper_ref[...]], axis=1
    )
    extended = jnp.concatenate(halves(extended), axis=0)
    width = extended.shape[1]
    out_ref[...] = inner_ref[...]
    left[...] = jnp.zeros_like(left)
    empty = jnp.zeros((8, count), f32)
    for f in range(4):
        pick = flags(iota((width, count), 0) == neighbor_ref[f : f + 1, :]).astype(bf16)
        found = product(extended, pick)
        found = found[0:216] + found[216:432]
        for a in range(12):
            left[a * 24 : a * 24 + 20, 0:20] = flux_ref[a, :, f, :]
        packed = pack_left(left[...])
        turn = orientation_ref[f : f + 1, :]
        for q in range(9):
            mine = jnp.concatenate([found[q * 24 : q * 24 + 24], empty], axis=0)
            every = product(packed, pack_right(mine))
            chosen = every[0:24]
            for a in range(1, 12):
                chosen = jnp.where(turn == a, every[a * 24 : a * 24 + 24], chosen)
            moved[q] = chosen

        def tile(i, carry):
            lanes = pl.ds(pl.multiple_of(i * 128, 128), 128)
            total = [out_ref[p, :, lanes] for p in range(9)]
            for q in range(9):
                part = moved[q, :, lanes]
                for p in range(9):
                    total[p] = total[p] - plus_ref[q, p, f : f + 1, lanes] * part
            for p in range(9):
                out_ref[p, :, lanes] = total[p]
            return carry

        lax.fori_loop(0, count // 128, tile, 0)


def face_expand(face_ref, pad):
    pad[...] = jnp.zeros_like(pad)
    pad[0:10, 0:25] = face_ref[...]
    row = iota((32, 16), 0)
    pick = flags((row - 10 * thirds(row) == iota((32, 16), 1)) & (row < 30))
    spread = flags((iota((128, 96), 1) & 31) == iota((128, 96), 0))
    wide = product_full(product_full(pick, pad[...]), spread)
    return jnp.where((iota((32, 96), 1) >> 5) == thirds(iota((32, 96), 0)), wide, 0.0)


def friction_kernel(
    arrived_ref,
    position_ref,
    owner_ref,
    impedance_ref,
    eval_ref,
    weight_ref,
    normal_ref,
    shear_ref,
    slip_ref,
    static_ref,
    drop_ref,
    scale_ref,
    reply_ref,
    slip_out_ref,
    traction_ref,
    pad,
    states,
):
    owned = owner_flags(owner_ref).astype(bf16)
    position = position_ref[0:1, :]
    faults = slip_ref.shape[1]
    wave = jnp.zeros((32, 2 * faults), f32)
    for r in range(6):
        high, low = halves(arrived_ref[pl.ds(r, 128, stride=8), :].T)
        found = product(jnp.concatenate([high, low], axis=0), owned)
        found = found[0:128] + found[128:256]
        for j in range(4):
            wave = jnp.where(position == float(4 * r + j), found[j * 32 : j * 32 + 32], wave)
    pwave_minus = impedance_ref[0:1, :]
    pwave_plus = impedance_ref[1:2, :]
    swave_minus = impedance_ref[2:3, :]
    swave_plus = impedance_ref[3:4, :]
    pwave_sum = pwave_minus + pwave_plus
    swave_sum = swave_minus + swave_plus
    viscous = swave_minus * swave_plus / swave_sum
    normal_row = iota((32, faults), 0) < 10
    modal = (
        jnp.where(normal_row, pwave_plus / pwave_sum, swave_plus / swave_sum) * wave[:, 0:faults]
        + jnp.where(normal_row, pwave_minus / pwave_sum, swave_minus / swave_sum)
        * wave[:, faults : 2 * faults]
    ) * (1.0 / time_step)
    evaluate = face_expand(eval_ref, pad)
    states[...] = product_full(evaluate, modal, 0, 0)
    normal = states[0:25, :]
    initial = (shear_ref[:, 0, :], shear_ref[:, 1, :])
    shear = (states[32:57, :] + initial[0], states[64:89, :] + initial[1])
    weakened = jnp.minimum(slip_ref[...] / scale_ref[...], 1.0)
    coefficient = static_ref[...] - drop_ref[...] * weakened
    strength = coefficient * jnp.maximum(-(normal + normal_ref[...]), 0.0)
    magnitude = jnp.sqrt(shear[0] * shear[0] + shear[1] * shear[1])
    ratio = jnp.minimum(1.0, strength / jnp.maximum(magnitude, 1.0))
    final = (shear[0] * ratio, shear[1] * ratio)
    rate_0 = (shear[0] - final[0]) / viscous
    rate_1 = (shear[1] - final[1]) / viscous
    slip_out_ref[...] = slip_ref[...] + time_step * jnp.sqrt(rate_0 * rate_0 + rate_1 * rate_1)
    traction_ref[:, 0, :] = final[0]
    traction_ref[:, 1, :] = final[1]
    states[32:57, :] = final[0] - initial[0]
    states[64:89, :] = final[1] - initial[1]
    weight = face_expand(weight_ref, pad)
    imposed = product_full(weight, states[...])
    high = imposed.astype(bf16).astype(f32)
    low = imposed - high
    high = jnp.concatenate([high, high], axis=1)
    low = jnp.concatenate([low, low], axis=1)
    for r in range(6):
        here = [position == float(4 * r + j) for j in range(4)]
        rows = jnp.concatenate(
            [jnp.where(here[j], high, 0.0).astype(bf16) for j in range(4)]
            + [jnp.where(here[j], low, 0.0).astype(bf16) for j in range(4)],
            axis=0,
        )
        block = product(rows, owned, 1, 1)
        reply_ref[pl.ds(r, 128, stride=8), :] = (block[0:128] + block[128:256]).T
    for r in range(6, 8):
        reply_ref[pl.ds(r, 128, stride=8), :] = jnp.zeros((128, 128), f32)


def final_kernel(
    request_ref,
    returned_ref,
    modal_ref,
    lift_ref,
    dofs_ref,
    partial_ref,
    eval_ref,
    weight_ref,
    out_ref,
    pad,
    totals,
):
    count = dofs_ref.shape[2]
    request = request_ref[...]
    element, _ = slots_of(request)
    turned = request.T
    _, face = slots_of(turned)
    inverse = jnp.where(turned == 0.0, 0.0, 1.0 / jnp.where(turned == 0.0, 1.0, turned))
    row = iota((32, 128), 0)
    normal_row = (row < 10) | (row == 30)
    for r in range(6):
        block = returned_ref[pl.ds(r, 128, stride=8), :].T
        highs = []
        lows = []
        for j in range(4):
            k = 4 * r + j
            plain = jnp.where(row >= 30, 1.0, block[j * 32 : j * 32 + 32])
            scale = jnp.where(normal_row, inverse[24 + k : 25 + k, :], inverse[48 + k : 49 + k, :])
            mine = jnp.concatenate([plain, plain * scale], axis=0)
            side = face[k : k + 1, :]
            mine = jnp.concatenate([jnp.where(side == f, mine, 0.0) for f in range(4)], axis=0)
            high, low = halves(mine)
            highs.append(high)
            lows.append(low)
        values = jnp.concatenate(
            [jnp.concatenate(highs, axis=1), jnp.concatenate(lows, axis=1)], axis=0
        )
        pick = slot_flags(element, 4 * r, 4, count)
        part = product(values, pick)
        part = part[0:256] + part[256:512]
        if r:
            totals[...] += part
        else:
            totals[...] = part
    evaluate = face_expand(eval_ref, pad)
    weight = face_expand(weight_ref, pad)
    gauss = product_full(weight, evaluate, 1, 1) * (1.0 / time_step)
    row = iota((32, count), 0) < 10
    states = []
    for f in range(4):
        base = f * 64
        own = product_full(gauss, modal_ref[base : base + 32, :])
        sides = totals[base + 30 : base + 31, :]
        scaled = jnp.where(row, totals[base + 62 : base + 63, :], totals[base + 63 : base + 64, :])
        states.append(totals[base : base + 32, :] - sides * own)
        states.append(totals[base + 32 : base + 64, :] - scaled * own)
    fault = product_full(lift_ref[...], jnp.concatenate(states, axis=0), 0, 0)
    for p in range(9):
        value = dofs_ref[p] + partial_ref[p, 0:20, :]
        if p in trace_rows:
            k = trace_rows.index(p)
            value = value + fault[k * 32 : k * 32 + 20, :]
        out_ref[p] = value


def call(kernel, name, outs, scratch, operands, flops):
    return pl.pallas_call(
        kernel,
        name=name,
        out_shape=[jax.ShapeDtypeStruct(shape, f32) for shape in outs],
        in_specs=[vmem] * len(operands),
        out_specs=[vmem] * len(outs),
        scratch_shapes=[pltpu.VMEM(shape, f32) for shape in scratch],
        compiler_params=pltpu.CompilerParams(vmem_limit_bytes=48 * 1024 * 1024),
        cost_estimate=pl.CostEstimate(flops=flops, bytes_accessed=4_000_000, transcendentals=0),
    )(*operands)


def exchange(block):
    return lax.all_to_all(block, both, split_axis=0, concat_axis=0, tiled=True)


def per_device(
    dofs,
    star,
    stiff,
    flux_local,
    flux_neighbor,
    solver_minus,
    solver_plus,
    neighbor,
    orientation,
    copy_list,
    face_lift,
    face_eval,
    face_weight,
    side_owner,
    side_face,
    impedance,
    normal_initial,
    shear_initial,
    slip,
    static_friction,
    friction_drop,
    slip_scale,
):
    count = dofs.shape[2]
    faults = side_owner.shape[0]
    owner = jnp.transpose(side_owner)
    wanted = jnp.transpose(side_face)
    star = jnp.transpose(star, (1, 2, 0, 3))
    minus = jnp.transpose(solver_minus, (1, 2, 0, 3))
    plus = jnp.transpose(solver_plus, (1, 2, 0, 3))
    local = jnp.transpose(flux_local, (1, 0, 2))
    flux = jnp.transpose(flux_neighbor, (1, 2, 0, 3))
    lift = jnp.transpose(face_lift, (1, 0, 2))
    evaluate = jnp.transpose(face_eval)
    shear = jnp.transpose(shear_initial, (1, 0, 2))
    request, position = call(
        request_kernel,
        "request",
        [(128, 128), (8, 2 * faults)],
        [],
        [owner, wanted, impedance],
        10**8,
    )
    asked = exchange(request.reshape(128, 1, 128)).reshape(128, 128)
    integral, modal, table, spread, low, up = call(
        predictor_kernel,
        "predictor",
        [(9, 24, count), (256, count), (count, 256), (256, 192), (216, 128), (216, 128)],
        [(9, 32, count), (9, 96, count), (96, 128), (64, 128)],
        [dofs, star, stiff, lift, copy_list],
        10**10,
    )
    (payload,) = call(
        gather_kernel, "gather", [(1024, 128)], [], [asked, table], 10**9
    )
    arrived = exchange(payload.reshape(128, 8, 128)).reshape(1024, 128)
    from_lower = from_behind(up, both, 1)
    from_upper = from_behind(low, both, -1)
    (inner,) = call(
        inner_kernel,
        "inner",
        [(9, 24, count)],
        [(224, 128), (128, 128), (9, 224, count)],
        [integral, star, minus, stiff, local],
        10**10,
    )
    reply, new_slip, traction = call(
        friction_kernel,
        "friction",
        [(1024, 128), (25, faults), (25, 2, faults)],
        [(16, 128), (96, faults)],
        [
            arrived,
            position,
            owner,
            impedance,
            evaluate,
            face_weight,
            normal_initial,
            shear,
            slip,
            static_friction,
            friction_drop,
            slip_scale,
        ],
        10**9,
    )
    returned = exchange(reply.reshape(128, 8, 128)).reshape(1024, 128)
    (partial,) = call(
        neighbour_kernel,
        "neighbour",
        [(9, 24, count)],
        [(288, 128), (9, 24, count)],
        [inner, integral, from_lower, from_upper, neighbor, orientation, plus, flux],
        10**10,
    )
    (new_dofs,) = call(
        final_kernel,
        "final",
        [(9, 20, count)],
        [(16, 128), (256, count)],
        [asked, returned, modal, spread, dofs, partial, evaluate, face_weight],
        10**9,
    )
    return (new_dofs, new_slip, jnp.transpose(traction, (1, 0, 2)))


def solution(mesh):
    in_specs = (
        P(None, None, ("dom", "sub")),
        P(None, None, None, ("dom", "sub")),
        P(),
        P(),
        P(),
        P(None, None, None, ("dom", "sub")),
        P(None, None, None, ("dom", "sub")),
        P(None, ("dom", "sub")),
        P(None, ("dom", "sub")),
        P(None, ("dom", "sub")),
        P(),
        P(),
        P(),
        P(("dom", "sub"), None),
        P(("dom", "sub"), None),
        P(None, ("dom", "sub")),
        P(None, ("dom", "sub")),
        P(None, None, ("dom", "sub")),
        P(None, ("dom", "sub")),
        P(None, ("dom", "sub")),
        P(None, ("dom", "sub")),
        P(None, ("dom", "sub")),
    )
    out_specs = (
        P(None, None, ("dom", "sub")),
        P(None, ("dom", "sub")),
        P(None, None, ("dom", "sub")),
    )
    return jax.shard_map(
        per_device, mesh=mesh, in_specs=in_specs, out_specs=out_specs, check_vma=False
    )
```

```python
import jax
import jax.numpy as jnp
from jax import lax
from jax.experimental import pallas as pl
from jax.experimental.pallas import tpu as pltpu
from jax.sharding import PartitionSpec as P

time_step = 0.8
trace_rows = (0, 3, 5, 6, 7, 8)
both = ("dom", "sub")
f32 = jnp.float32
bf16 = jnp.bfloat16
vmem = pl.BlockSpec(memory_space=pltpu.VMEM)


def from_behind(block, axis, distance):
    devices = range(lax.axis_size(axis))
    route = [(i - distance, i) for i in devices if i - distance in devices]
    return lax.ppermute(block, axis, route)


def iota(shape, axis):
    return lax.broadcasted_iota(jnp.int32, shape, axis)


def product(a, b, left=1, right=0):
    return lax.dot_general(a, b, (((left,), (right,)), ((), ())), preferred_element_type=f32)


def product_full(a, b, left=1, right=0):
    return lax.dot_general(
        a,
        b,
        (((left,), (right,)), ((), ())),
        precision=lax.Precision.HIGHEST,
        preferred_element_type=f32,
    )


def halves(x):
    high = x.astype(bf16)
    low = (x - high.astype(f32)).astype(bf16)
    return high, low


def flags(condition):
    return jnp.where(condition, 1.0, 0.0).astype(f32)


def pack_left(a):
    wide = a + pltpu.roll(a, 32, 1)
    wide = wide + pltpu.roll(wide, 64, 1)
    high = wide.astype(bf16).astype(f32)
    return jnp.where(iota(wide.shape, 1) < 64, high, wide - high).astype(bf16)


def pack_right(x):
    high, low = halves(x)
    return jnp.concatenate([high, low, high, low], axis=0)


def thirds(t):
    return jnp.where(t >= 10, 1, 0) + jnp.where(t >= 20, 1, 0)


def owner_flags(owner_ref):
    owner = jnp.concatenate([owner_ref[0:1, :], owner_ref[1:2, :]], axis=1)
    return flags(iota((128, owner.shape[1]), 0) == owner)


def request_kernel(owner_late, face_late, impedance_late, request_ref, position_ref):
    owned = owner_flags(owner_late.get())
    owned_half = owned.astype(bf16)
    sides = owned.shape[1]
    block = 256
    ahead = flags(iota((block, block), 0) < iota((block, block), 1)).astype(bf16)
    carry = jnp.zeros((128, 1), f32)
    positions = []
    for start in range(0, sides, block):
        part = owned[:, start : start + block]
        before = product(owned_half[:, start : start + block], ahead) + carry
        positions.append(jnp.sum(part * before, axis=0, keepdims=True))
        carry = carry + jnp.sum(part, axis=1, keepdims=True)
    position = jnp.concatenate(positions, axis=1)
    position_ref[...] = jnp.broadcast_to(position, position_ref.shape)
    face_ref = face_late.get()
    impedance_ref = impedance_late.get()
    wanted = jnp.concatenate([face_ref[0:1, :], face_ref[1:2, :]], axis=1).astype(f32) + 1.0
    zp = jnp.concatenate([impedance_ref[0:1, :], -impedance_ref[1:2, :]], axis=1)
    zs = jnp.concatenate([impedance_ref[2:3, :], -impedance_ref[3:4, :]], axis=1)
    row = iota((128, sides), 0)
    channel = jnp.where(row >= 24, 1, 0) + jnp.where(row >= 48, 1, 0)
    slot = (row - 24 * channel).astype(f32)
    value = jnp.where(row < 24, wanted, jnp.where(row < 48, zp, zs))
    value = jnp.where((slot == position) & (row < 72), value, 0.0)
    high = value.astype(bf16)
    rest = value - high.astype(f32)
    middle, low = halves(rest)
    request_ref[...] = (
        product(owned_half, high, 1, 1)
        + product(owned_half, middle, 1, 1)
        + product(owned_half, low, 1, 1)
    )


def lift_expand(lift_ref, pad, wide):
    pad[...] = jnp.zeros_like(pad)
    wide[...] = jnp.zeros_like(wide)
    for face in range(4):
        pad[0:10, 0:20] = lift_ref[:, face, :]
        block = pad[...]
        for k in range(6):
            first = face * 64 + (k // 3) * 32 + (k % 3) * 10
            lane = k // 4 * 128
            moved = pltpu.roll(block, 32 * (k % 4), 1) if k % 4 else block
            wide[first : first + 10, lane : lane + 128] = moved[0:10]
    return wide[...]


def face_expand(face_ref, pad, wide):
    pad[...] = jnp.zeros_like(pad)
    wide[...] = jnp.zeros_like(wide)
    pad[0:10, 0:25] = face_ref[...]
    block = pad[...]
    for j in range(3):
        moved = pltpu.roll(block, 32 * j, 1) if j else block
        wide[j * 10 : j * 10 + 10, :] = moved[0:10]
    return wide[:, 0:96]


def predictor_kernel(
    dofs_ref,
    star_ref,
    stiff_ref,
    lift_ref,
    integral_ref,
    modal_ref,
    current,
    moved,
    left,
    pad,
    wide,
):
    count = dofs_ref.shape[2]
    left[...] = jnp.zeros_like(left)
    for d in range(3):
        left[d * 32 : d * 32 + 20, 0:20] = stiff_ref[d]
    packed = pack_left(left[...])
    current[...] = jnp.zeros_like(current)
    for q in range(9):
        current[q, 0:20, :] = dofs_ref[q]
        integral_ref[q, :, :] = time_step * current[q, 0:24, :]
    factor = time_step
    for order in range(1, 4):
        factor = factor * time_step / (order + 1)
        for q in range(9):
            moved[q] = product(packed, pack_right(current[q]))

        def tile(i, carry):
            lanes = pl.ds(pl.multiple_of(i * 128, 128), 128)
            total = [jnp.zeros((24, 128), f32) for _ in range(9)]
            for q in range(9):
                for d in range(3):
                    part = moved[q, d * 32 : d * 32 + 24, lanes]
                    for p in range(9):
                        total[p] = total[p] - star_ref[q, p, d : d + 1, lanes] * part
            for p in range(9):
                current[p, 0:24, lanes] = total[p]
                integral_ref[p, :, lanes] += factor * total[p]
            return carry

        lax.fori_loop(0, count // 128, tile, 0)
    spread = lift_expand(lift_ref, pad, wide)[:, 0:192]
    for p in range(9):
        current[p, 0:24, :] = integral_ref[p]
    rows = jnp.concatenate([current[r] for r in trace_rows], axis=0)
    rows_high, rows_low = halves(rows)
    spread_high, spread_low = halves(spread)
    modal = (
        product(spread_high, rows_high)
        + product(spread_high, rows_low)
        + product(spread_low, rows_high)
    )
    modal_ref[...] = modal


def slots_of(request):
    wanted = (request + 0.5).astype(jnp.int32) - 1
    element = jnp.where(wanted < 0, -1, wanted & 511)
    return element, wanted >> 9


def slot_flags(element, first, many, count):
    row = iota((count, 128), 0)
    return jnp.concatenate(
        [flags(element[k : k + 1, :] == row).astype(bf16) for k in range(first, first + many)],
        axis=1,
    )


def gather_kernel(request_ref, modal_ref, out_ref):
    turned = request_ref[...].T
    element, face = slots_of(turned)
    modal = jnp.concatenate(halves(modal_ref[...]), axis=0)
    normal_row = iota((32, 128), 0) < 10
    for r in range(6):
        pick = slot_flags(element, 4 * r, 4, modal_ref.shape[1])
        found = product(modal, pick)
        found = found[0:256] + found[256:512]
        waves = []
        for j in range(4):
            k = 4 * r + j
            mine = found[:, j * 128 : j * 128 + 128]
            side = face[k : k + 1, :]
            state = mine[0:64]
            for f in range(1, 4):
                state = jnp.where(side == f, mine[f * 64 : f * 64 + 64], state)
            z = jnp.where(normal_row, turned[24 + k : 25 + k, :], turned[48 + k : 49 + k, :])
            waves.append(state[0:32] - z * state[32:64])
        out_ref[pl.ds(r, 128, stride=6), :] = jnp.concatenate(waves, axis=0).T


def inner_kernel(
    integral_ref,
    dofs_ref,
    star_ref,
    minus_ref,
    stiff_ref,
    local_ref,
    copy_ref,
    out_ref,
    low_ref,
    up_ref,
    left,
    square,
    moved,
):
    left[...] = jnp.zeros_like(left)
    square[...] = jnp.zeros_like(square)
    for d in range(3):
        square[0:20, 0:20] = stiff_ref[d]
        left[d * 32 : d * 32 + 32, :] = square[...].T[0:32, :]
    for f in range(4):
        left[96 + f * 32 : 96 + f * 32 + 20, 0:20] = local_ref[:, f, :]
    packed = pack_left(left[...])
    count = integral_ref.shape[2]
    whole = jnp.concatenate(halves(integral_ref[...].reshape(216, count)), axis=0)
    wanted = jnp.concatenate([copy_ref[0:1, :], copy_ref[1:2, :]], axis=1)
    found = product(whole, flags(iota((count, 256), 0) == wanted).astype(bf16))
    found = found[0:216] + found[216:432]
    low_ref[...] = found[:, 0:128]
    up_ref[...] = found[:, 128:256]
    empty = jnp.zeros((8, count), f32)
    for q in range(9):
        moved[q] = product(
            packed, pack_right(jnp.concatenate([integral_ref[q], empty], axis=0))
        )

    def tile(i, carry):
        lanes = pl.ds(pl.multiple_of(i * 128, 128), 128)
        total = [jnp.zeros((24, 128), f32) for _ in range(9)]
        for q in range(9):
            for d in range(3):
                part = moved[q, d * 32 : d * 32 + 24, lanes]
                for p in range(9):
                    total[p] = total[p] + star_ref[q, p, d : d + 1, lanes] * part
            for f in range(4):
                part = moved[q, 96 + f * 32 : 96 + f * 32 + 24, lanes]
                for p in range(9):
                    total[p] = total[p] - minus_ref[q, p, f : f + 1, lanes] * part
        for p in range(9):
            out_ref[p, :, lanes] = total[p]
        return carry

    lax.fori_loop(0, count // 128, tile, 0)
    for p in range(9):
        out_ref[p, 0:20, :] += dofs_ref[p]


def neighbour_kernel(
    inner_ref,
    integral_ref,
    lower_ref,
    upper_ref,
    neighbor_ref,
    orientation_ref,
    plus_ref,
    flux_ref,
    lift_ref,
    eval_ref,
    weight_ref,
    out_ref,
    own_ref,
    spread_ref,
    left,
    moved,
    pad,
    wide,
    face_wide,
):
    count = integral_ref.shape[2]
    evaluate = face_expand(eval_ref, pad, face_wide)
    weight = face_expand(weight_ref, pad, face_wide)
    gauss = product_full(weight, evaluate, 1, 1) * (1.0 / time_step)
    spread = lift_expand(lift_ref, pad, wide)
    spread_ref[...] = spread.T[0:192, :]
    outer = jnp.concatenate(
        [product_full(gauss, spread[f * 64 : f * 64 + 32, 0:128]) for f in range(4)], axis=0
    )
    empty = jnp.zeros((8, count), f32)
    rows = [jnp.concatenate([integral_ref[r], empty], axis=0) for r in trace_rows[0:3]]
    own_ref[...] = product_full(outer[:, 0:96], jnp.concatenate(rows, axis=0))
    extended = jnp.concatenate(
        [integral_ref[...].reshape(216, count), lower_ref[...], upper_ref[...]], axis=1
    )
    extended = jnp.concatenate(halves(extended), axis=0)
    width = extended.shape[1]
    out_ref[...] = inner_ref[...]
    left[...] = jnp.zeros_like(left)
    for f in range(4):
        pick = flags(iota((width, count), 0) == neighbor_ref[f : f + 1, :]).astype(bf16)
        found = product(extended, pick)
        found = found[0:216] + found[216:432]
        for a in range(12):
            left[a * 24 : a * 24 + 20, 0:20] = flux_ref[a, :, f, :]
        packed = pack_left(left[...])
        turn = orientation_ref[f : f + 1, :]
        for q in range(9):
            mine = jnp.concatenate([found[q * 24 : q * 24 + 24], empty], axis=0)
            every = product(packed, pack_right(mine))
            chosen = every[0:24]
            for a in range(1, 12):
                chosen = jnp.where(turn == a, every[a * 24 : a * 24 + 24], chosen)
            moved[q] = chosen

        def tile(i, carry):
            lanes = pl.ds(pl.multiple_of(i * 128, 128), 128)
            total = [out_ref[p, :, lanes] for p in range(9)]
            for q in range(9):
                part = moved[q, :, lanes]
                for p in range(9):
                    total[p] = total[p] - plus_ref[q, p, f : f + 1, lanes] * part
            for p in range(9):
                out_ref[p, :, lanes] = total[p]
            return carry

        lax.fori_loop(0, count // 128, tile, 0)


def friction_kernel(
    arrived_ref,
    position_ref,
    owner_ref,
    impedance_ref,
    eval_ref,
    weight_ref,
    normal_ref,
    shear_ref,
    slip_ref,
    static_ref,
    drop_ref,
    scale_ref,
    reply_ref,
    slip_out_ref,
    traction_ref,
    states,
    pad,
    face_wide,
):
    owned = owner_flags(owner_ref).astype(bf16)
    owned_twice = jnp.concatenate([owned, owned], axis=0)
    position = position_ref[0:1, :]
    faults = slip_ref.shape[1]
    wave = jnp.zeros((32, 2 * faults), f32)
    for r in range(6):
        high, low = halves(arrived_ref[pl.ds(r, 128, stride=6), :].T)
        found = product(jnp.concatenate([high, low], axis=1), owned_twice)
        for j in range(4):
            wave = jnp.where(position == float(4 * r + j), found[j * 32 : j * 32 + 32], wave)
    pwave_minus = impedance_ref[0:1, :]
    pwave_plus = impedance_ref[1:2, :]
    swave_minus = impedance_ref[2:3, :]
    swave_plus = impedance_ref[3:4, :]
    pwave_sum = pwave_minus + pwave_plus
    swave_sum = swave_minus + swave_plus
    viscous = swave_minus * swave_plus / swave_sum
    normal_row = iota((32, faults), 0) < 10
    modal = (
        jnp.where(normal_row, pwave_plus / pwave_sum, swave_plus / swave_sum) * wave[:, 0:faults]
        + jnp.where(normal_row, pwave_minus / pwave_sum, swave_minus / swave_sum)
        * wave[:, faults : 2 * faults]
    ) * (1.0 / time_step)
    states[...] = product_full(face_expand(eval_ref, pad, face_wide), modal, 0, 0)
    normal = states[0:25, :]
    initial = (shear_ref[:, 0, :], shear_ref[:, 1, :])
    shear = (states[32:57, :] + initial[0], states[64:89, :] + initial[1])
    weakened = jnp.minimum(slip_ref[...] / scale_ref[...], 1.0)
    coefficient = static_ref[...] - drop_ref[...] * weakened
    strength = coefficient * jnp.maximum(-(normal + normal_ref[...]), 0.0)
    magnitude = jnp.sqrt(shear[0] * shear[0] + shear[1] * shear[1])
    ratio = jnp.minimum(1.0, strength / jnp.maximum(magnitude, 1.0))
    final = (shear[0] * ratio, shear[1] * ratio)
    rate_0 = (shear[0] - final[0]) / viscous
    rate_1 = (shear[1] - final[1]) / viscous
    slip_out_ref[...] = slip_ref[...] + time_step * jnp.sqrt(rate_0 * rate_0 + rate_1 * rate_1)
    traction_ref[:, 0, :] = final[0]
    traction_ref[:, 1, :] = final[1]
    states[32:57, :] = final[0] - initial[0]
    states[64:89, :] = final[1] - initial[1]
    imposed = product_full(face_expand(weight_ref, pad, face_wide), states[...])
    high = imposed.astype(bf16).astype(f32)
    low = imposed - high
    high = jnp.concatenate([high, high], axis=1)
    low = jnp.concatenate([low, low], axis=1)
    rows = []
    for k in range(24):
        here = position == float(k)
        rows.append(jnp.where(here, high, 0.0).astype(bf16))
        rows.append(jnp.where(here, low, 0.0).astype(bf16))
    blocks = product(jnp.concatenate(rows, axis=0), owned, 1, 1)
    for r in range(6):
        parts = [blocks[k * 64 : k * 64 + 32] + blocks[k * 64 + 32 : k * 64 + 64] for k in range(4 * r, 4 * r + 4)]
        reply_ref[pl.ds(r, 128, stride=6), :] = jnp.concatenate(parts, axis=0).T


def final_kernel(
    request_ref,
    returned_ref,
    own_ref,
    spread_ref,
    partial_ref,
    out_ref,
    totals,
):
    count = partial_ref.shape[2]
    request = request_ref[...]
    turned = request.T
    element, face = slots_of(turned)
    inverse = jnp.where(turned == 0.0, 0.0, 1.0 / jnp.where(turned == 0.0, 1.0, turned))
    row = iota((32, 128), 0)
    normal_row = (row < 10) | (row == 30)
    for r in range(6):
        block = returned_ref[pl.ds(r, 128, stride=6), :].T
        highs = []
        lows = []
        for j in range(4):
            k = 4 * r + j
            plain = jnp.where(row >= 30, 1.0, block[j * 32 : j * 32 + 32])
            scale = jnp.where(normal_row, inverse[24 + k : 25 + k, :], inverse[48 + k : 49 + k, :])
            mine = jnp.concatenate([plain, plain * scale], axis=0)
            side = face[k : k + 1, :]
            mine = jnp.concatenate([jnp.where(side == f, mine, 0.0) for f in range(4)], axis=0)
            high, low = halves(mine)
            highs.append(high)
            lows.append(low)
        values = jnp.concatenate(
            [jnp.concatenate(highs, axis=1), jnp.concatenate(lows, axis=1)], axis=0
        )
        pick = slot_flags(element, 4 * r, 4, count)
        part = product(values, pick, 1, 1)
        part = part[0:256] + part[256:512]
        if r:
            totals[...] += part
        else:
            totals[...] = part
    row = iota((32, count), 0) < 10
    states = []
    for f in range(4):
        base = f * 64
        own = own_ref[f * 32 : f * 32 + 32, :]
        sides = totals[base + 30 : base + 31, :]
        scaled = jnp.where(row, totals[base + 62 : base + 63, :], totals[base + 63 : base + 64, :])
        states.append(totals[base : base + 32, :] - sides * own)
        states.append(totals[base + 32 : base + 64, :] - scaled * own)
    high, low = halves(jnp.concatenate(states, axis=0))
    spread_high, spread_low = halves(spread_ref[...])
    fault = product(
        jnp.concatenate([spread_high, spread_high, spread_low], axis=1),
        jnp.concatenate([high, low, high], axis=0),
    )
    for p in range(9):
        value = partial_ref[p, 0:20, :]
        if p in trace_rows:
            k = trace_rows.index(p)
            value = value + fault[k * 32 : k * 32 + 20, :]
        out_ref[p] = value


class Arriving:
    def __init__(self, copy, ref):
        self.copy = copy
        self.ref = ref

    def get(self):
        self.copy.wait()
        return self.ref


def call(kernel, name, outs, scratch, operands, flops, late=(), room=20):
    inputs = len(operands)
    outputs = len(outs)
    own = len(scratch)

    def body(*refs):
        sources = list(refs[:inputs])
        spare = refs[inputs + outputs + own : -1]
        flags_ref = refs[-1]
        for index, place in enumerate(late):
            copy = pltpu.make_async_copy(sources[place], spare[index], flags_ref.at[index])
            copy.start()
            sources[place] = Arriving(copy, spare[index])
        kernel(*sources, *refs[inputs : inputs + outputs + own])

    far = pl.BlockSpec(memory_space=pltpu.HBM)
    return pl.pallas_call(
        body,
        name=name,
        out_shape=[jax.ShapeDtypeStruct(shape, f32) for shape in outs],
        in_specs=[far if i in late else vmem for i in range(inputs)],
        out_specs=[vmem] * outputs,
        scratch_shapes=[pltpu.VMEM(shape, f32) for shape in scratch]
        + [pltpu.VMEM(operands[i].shape, operands[i].dtype) for i in late]
        + [pltpu.SemaphoreType.DMA((max(1, len(late)),))],
        compiler_params=pltpu.CompilerParams(vmem_limit_bytes=room * 1024 * 1024),
        cost_estimate=pl.CostEstimate(flops=flops, bytes_accessed=4_000_000, transcendentals=0),
    )(*operands)


def exchange(block):
    return lax.all_to_all(block, both, split_axis=0, concat_axis=0, tiled=True)


def per_device(
    dofs,
    star,
    stiff,
    flux_local,
    flux_neighbor,
    solver_minus,
    solver_plus,
    neighbor,
    orientation,
    copy_list,
    face_lift,
    face_eval,
    face_weight,
    side_owner,
    side_face,
    impedance,
    normal_initial,
    shear_initial,
    slip,
    static_friction,
    friction_drop,
    slip_scale,
):
    count = dofs.shape[2]
    faults = side_owner.shape[0]
    owner = jnp.transpose(side_owner)
    wanted = jnp.transpose(side_face)
    star = jnp.transpose(star, (1, 2, 0, 3))
    minus = jnp.transpose(solver_minus, (1, 2, 0, 3))
    plus = jnp.transpose(solver_plus, (1, 2, 0, 3))
    local = jnp.transpose(flux_local, (1, 0, 2))
    flux = jnp.transpose(flux_neighbor, (1, 2, 0, 3))
    lift = jnp.transpose(face_lift, (1, 0, 2))
    evaluate = jnp.transpose(face_eval)
    shear = jnp.transpose(shear_initial, (1, 0, 2))
    request, position = call(
        request_kernel,
        "request",
        [(128, 128), (8, 2 * faults)],
        [],
        [owner, wanted, impedance],
        10**8,
        late=(0, 1, 2),
        room=60,
    )
    asked = exchange(request.reshape(128, 1, 128)).reshape(128, 128)
    integral, modal = call(
        predictor_kernel,
        "predictor",
        [(9, 24, count), (256, count)],
        [(9, 32, count), (9, 96, count), (96, 128), (16, 128), (256, 256)],
        [dofs, star, stiff, lift],
        10**10,
    )
    (payload,) = call(gather_kernel, "gather", [(768, 128)], [], [asked, modal], 10**9)
    arrived = exchange(payload.reshape(128, 1, 768)).reshape(768, 128)
    inner, low, up = call(
        inner_kernel,
        "inner",
        [(9, 24, count), (216, 128), (216, 128)],
        [(224, 128), (128, 128), (9, 224, count)],
        [integral, dofs, star, minus, stiff, local, copy_list],
        10**10,
    )
    from_lower = from_behind(up, both, 1)
    from_upper = from_behind(low, both, -1)
    reply, new_slip, traction = call(
        friction_kernel,
        "friction",
        [(768, 128), (25, faults), (25, 2, faults)],
        [(96, faults), (16, 128), (32, 128)],
        [
            arrived,
            position,
            owner,
            impedance,
            evaluate,
            face_weight,
            normal_initial,
            shear,
            slip,
            static_friction,
            friction_drop,
            slip_scale,
        ],
        10**9,
    )
    returned = exchange(reply.reshape(128, 1, 768)).reshape(768, 128)
    partial, own, spread = call(
        neighbour_kernel,
        "neighbour",
        [(9, 24, count), (128, count), (192, 256)],
        [(288, 128), (9, 24, count), (16, 128), (256, 256), (32, 128)],
        [
            inner,
            integral,
            from_lower,
            from_upper,
            neighbor,
            orientation,
            plus,
            flux,
            lift,
            evaluate,
            face_weight,
        ],
        10**10,
    )
    (new_dofs,) = call(
        final_kernel,
        "final",
        [(9, 20, count)],
        [(256, count)],
        [asked, returned, own, spread, partial],
        10**9,
    )
    return (new_dofs, new_slip, jnp.transpose(traction, (1, 0, 2)))


def solution(mesh):
    in_specs = (
        P(None, None, ("dom", "sub")),
        P(None, None, None, ("dom", "sub")),
        P(),
        P(),
        P(),
        P(None, None, None, ("dom", "sub")),
        P(None, None, None, ("dom", "sub")),
        P(None, ("dom", "sub")),
        P(None, ("dom", "sub")),
        P(None, ("dom", "sub")),
        P(),
        P(),
        P(),
        P(("dom", "sub"), None),
        P(("dom", "sub"), None),
        P(None, ("dom", "sub")),
        P(None, ("dom", "sub")),
        P(None, None, ("dom", "sub")),
        P(None, ("dom", "sub")),
        P(None, ("dom", "sub")),
        P(None, ("dom", "sub")),
        P(None, ("dom", "sub")),
    )
    out_specs = (
        P(None, None, ("dom", "sub")),
        P(None, ("dom", "sub")),
        P(None, None, ("dom", "sub")),
    )
    return jax.shard_map(
        per_device, mesh=mesh, in_specs=in_specs, out_specs=out_specs, check_vma=False
    )
```

```python
import jax
import jax.numpy as jnp
from jax import lax
from jax.experimental import pallas as pl
from jax.experimental.pallas import tpu as pltpu
from jax.sharding import PartitionSpec as P

time_step = 0.8
trace_rows = (0, 3, 5, 6, 7, 8)
both = ("dom", "sub")
f32 = jnp.float32
bf16 = jnp.bfloat16
vmem = pl.BlockSpec(memory_space=pltpu.VMEM)


def from_behind(block, axis, distance):
    devices = range(lax.axis_size(axis))
    route = [(i - distance, i) for i in devices if i - distance in devices]
    return lax.ppermute(block, axis, route)


def iota(shape, axis):
    return lax.broadcasted_iota(jnp.int32, shape, axis)


def product(a, b, left=1, right=0):
    return lax.dot_general(a, b, (((left,), (right,)), ((), ())), preferred_element_type=f32)


def product_full(a, b, left=1, right=0):
    return lax.dot_general(
        a,
        b,
        (((left,), (right,)), ((), ())),
        precision=lax.Precision.HIGHEST,
        preferred_element_type=f32,
    )


def halves(x):
    high = x.astype(bf16)
    low = (x - high.astype(f32)).astype(bf16)
    return high, low


def flags(condition):
    return jnp.where(condition, 1.0, 0.0).astype(f32)


def pack_left(a):
    wide = a + pltpu.roll(a, 32, 1)
    wide = wide + pltpu.roll(wide, 64, 1)
    high = wide.astype(bf16).astype(f32)
    return jnp.where(iota(wide.shape, 1) < 64, high, wide - high).astype(bf16)


def pack_right(x):
    high, low = halves(x)
    return jnp.concatenate([high, low, high, low], axis=0)


def thirds(t):
    return jnp.where(t >= 10, 1, 0) + jnp.where(t >= 20, 1, 0)


def owner_flags(owner_ref):
    owner = jnp.concatenate([owner_ref[0:1, :], owner_ref[1:2, :]], axis=1)
    return flags(iota((128, owner.shape[1]), 0) == owner)


def request_kernel(owner_late, face_late, impedance_late, request_ref, position_ref):
    owned = owner_flags(owner_late.get())
    owned_half = owned.astype(bf16)
    sides = owned.shape[1]
    block = 256
    ahead = flags(iota((block, block), 0) < iota((block, block), 1)).astype(bf16)
    carry = jnp.zeros((128, 1), f32)
    positions = []
    for start in range(0, sides, block):
        part = owned[:, start : start + block]
        before = product(owned_half[:, start : start + block], ahead) + carry
        positions.append(jnp.sum(part * before, axis=0, keepdims=True))
        carry = carry + jnp.sum(part, axis=1, keepdims=True)
    position = jnp.concatenate(positions, axis=1)
    position_ref[...] = jnp.broadcast_to(position, position_ref.shape)
    face_ref = face_late.get()
    impedance_ref = impedance_late.get()
    wanted = jnp.concatenate([face_ref[0:1, :], face_ref[1:2, :]], axis=1).astype(f32) + 1.0
    zp = jnp.concatenate([impedance_ref[0:1, :], -impedance_ref[1:2, :]], axis=1)
    zs = jnp.concatenate([impedance_ref[2:3, :], -impedance_ref[3:4, :]], axis=1)
    row = iota((128, sides), 0)
    channel = jnp.where(row >= 24, 1, 0) + jnp.where(row >= 48, 1, 0)
    slot = (row - 24 * channel).astype(f32)
    value = jnp.where(row < 24, wanted, jnp.where(row < 48, zp, zs))
    value = jnp.where((slot == position) & (row < 72), value, 0.0)
    high = value.astype(bf16)
    rest = value - high.astype(f32)
    middle, low = halves(rest)
    request_ref[...] = (
        product(owned_half, high, 1, 1)
        + product(owned_half, middle, 1, 1)
        + product(owned_half, low, 1, 1)
    )


def lift_expand(lift_ref, pad, wide):
    pad[...] = jnp.zeros_like(pad)
    wide[...] = jnp.zeros_like(wide)
    for face in range(4):
        pad[0:10, 0:20] = lift_ref[:, face, :]
        block = pad[...]
        for k in range(6):
            first = face * 64 + (k // 3) * 32 + (k % 3) * 10
            lane = k // 4 * 128
            moved = pltpu.roll(block, 32 * (k % 4), 1) if k % 4 else block
            wide[first : first + 10, lane : lane + 128] = moved[0:10]
    return wide[...]


def face_expand(face_ref, pad, wide):
    pad[...] = jnp.zeros_like(pad)
    wide[...] = jnp.zeros_like(wide)
    pad[0:10, 0:25] = face_ref[...]
    block = pad[...]
    for j in range(3):
        moved = pltpu.roll(block, 32 * j, 1) if j else block
        wide[j * 10 : j * 10 + 10, :] = moved[0:10]
    return wide[:, 0:96]


def pack_turns(flux_ref, packed_ref, turns):
    turns[...] = jnp.zeros_like(turns)
    lane = iota((96, 256), 1)
    lane = lane - jnp.where(lane >= 72, 72, 0) - jnp.where(lane >= 144, 72, 0)
    for f in range(4):
        wide = jnp.zeros((96, 256), f32)
        for n in range(3):
            for a in range(4):
                turns[n, a * 24 : a * 24 + 20, 0:20] = flux_ref[n * 4 + a, :, f, :]
            wide = wide + (pltpu.roll(turns[n], n * 72, 1) if n else turns[n])
        wide = wide + pltpu.roll(wide, 24, 1) + pltpu.roll(wide, 48, 1)
        high = wide.astype(bf16).astype(f32)
        packed_ref[f] = jnp.where(lane < 48, high, wide - high).astype(bf16)


def predictor_kernel(
    dofs_ref,
    star_ref,
    stiff_ref,
    lift_ref,
    copy_ref,
    integral_ref,
    modal_ref,
    low_ref,
    up_ref,
    current,
    moved,
    left,
    pad,
    wide,
):
    count = dofs_ref.shape[2]
    left[...] = jnp.zeros_like(left)
    for d in range(3):
        left[d * 32 : d * 32 + 20, 0:20] = stiff_ref[d]
    packed = pack_left(left[...])
    current[...] = jnp.zeros_like(current)
    for q in range(9):
        current[q, 0:20, :] = dofs_ref[q]
        integral_ref[q, :, :] = time_step * current[q, 0:24, :]
    factor = time_step
    for order in range(1, 4):
        factor = factor * time_step / (order + 1)
        for q in range(9):
            moved[q] = product(packed, pack_right(current[q]))

        def tile(i, carry):
            lanes = pl.ds(pl.multiple_of(i * 128, 128), 128)
            total = [jnp.zeros((24, 128), f32) for _ in range(9)]
            for q in range(9):
                for d in range(3):
                    part = moved[q, d * 32 : d * 32 + 24, lanes]
                    for p in range(9):
                        total[p] = total[p] - star_ref[q, p, d : d + 1, lanes] * part
            for p in range(9):
                current[p, 0:24, lanes] = total[p]
                integral_ref[p, :, lanes] += factor * total[p]
            return carry

        lax.fori_loop(0, count // 128, tile, 0)
    whole = jnp.concatenate(halves(integral_ref[...].reshape(216, count)), axis=0)
    wanted = jnp.concatenate([copy_ref[0:1, :], copy_ref[1:2, :]], axis=1)
    found = product(whole, flags(iota((count, 256), 0) == wanted).astype(bf16))
    found = found[0:216] + found[216:432]
    low_ref[...] = found[:, 0:128]
    up_ref[...] = found[:, 128:256]
    spread = lift_expand(lift_ref, pad, wide)[:, 0:192]
    for p in range(9):
        current[p, 0:24, :] = integral_ref[p]
    rows = jnp.concatenate([current[r] for r in trace_rows], axis=0)
    rows_high, rows_low = halves(rows)
    spread_high, spread_low = halves(spread)
    modal = (
        product(spread_high, rows_high)
        + product(spread_high, rows_low)
        + product(spread_low, rows_high)
    )
    modal_ref[...] = modal


def slots_of(request):
    wanted = (request + 0.5).astype(jnp.int32) - 1
    element = jnp.where(wanted < 0, -1, wanted & 511)
    return element, wanted >> 9


def slot_flags(element, first, many, count):
    row = iota((count, 128), 0)
    return jnp.concatenate(
        [flags(element[k : k + 1, :] == row).astype(bf16) for k in range(first, first + many)],
        axis=1,
    )


def gather_kernel(request_ref, modal_ref, out_ref):
    turned = request_ref[...].T
    element, face = slots_of(turned)
    modal = jnp.concatenate(halves(modal_ref[...]), axis=0)
    normal_row = iota((32, 128), 0) < 10
    for r in range(6):
        pick = slot_flags(element, 4 * r, 4, modal_ref.shape[1])
        found = product(modal, pick)
        found = found[0:256] + found[256:512]
        waves = []
        for j in range(4):
            k = 4 * r + j
            mine = found[:, j * 128 : j * 128 + 128]
            side = face[k : k + 1, :]
            state = mine[0:64]
            for f in range(1, 4):
                state = jnp.where(side == f, mine[f * 64 : f * 64 + 64], state)
            z = jnp.where(normal_row, turned[24 + k : 25 + k, :], turned[48 + k : 49 + k, :])
            waves.append(state[0:32] - z * state[32:64])
        out_ref[pl.ds(r, 128, stride=6), :] = jnp.concatenate(waves, axis=0).T


def inner_kernel(
    integral_ref,
    dofs_ref,
    star_ref,
    stiff_ref,
    flux_ref,
    low_ref,
    up_ref,
    out_sent,
    packed_ref,
    low_out_ref,
    up_out_ref,
    left,
    square,
    moved,
    turns,
):
    pack_turns(flux_ref, packed_ref, turns)
    out_ref = out_sent.ref
    left[...] = jnp.zeros_like(left)
    square[...] = jnp.zeros_like(square)
    for d in range(3):
        square[0:20, 0:20] = stiff_ref[d]
        left[d * 32 : d * 32 + 32, :] = square[...].T[0:32, :]
    packed = pack_left(left[...])
    count = integral_ref.shape[2]
    empty = jnp.zeros((8, count), f32)
    for q in range(9):
        moved[q] = product(
            packed, pack_right(jnp.concatenate([integral_ref[q], empty], axis=0))
        )

    def tile(i, carry):
        lanes = pl.ds(pl.multiple_of(i * 128, 128), 128)
        total = [dofs_ref[p, :, lanes] for p in range(9)]
        for q in range(9):
            for d in range(3):
                part = moved[q, d * 32 : d * 32 + 20, lanes]
                for p in range(9):
                    total[p] = total[p] + star_ref[q, p, d : d + 1, lanes] * part
        for p in range(9):
            out_ref[p, :, lanes] = total[p]
        return carry

    lax.fori_loop(0, count // 128, tile, 0, unroll=True)
    out_sent.send()


def neighbour_kernel(
    inner_late,
    integral_ref,
    lower_ref,
    upper_ref,
    neighbor_ref,
    orientation_ref,
    plus_ref,
    packed_ref,
    minus_ref,
    local_ref,
    lift_ref,
    eval_ref,
    weight_ref,
    out_sent,
    own_ref,
    spread_ref,
    left,
    moved,
    local_moved,
    pad,
    wide,
    face_wide,
):
    count = integral_ref.shape[2]
    out_ref = out_sent.ref
    empty = jnp.zeros((8, count), f32)
    left[...] = jnp.zeros_like(left)
    for f in range(4):
        left[f * 32 : f * 32 + 20, 0:20] = local_ref[:, f, :]
    packed = pack_left(left[...])
    for q in range(9):
        local_moved[q] = product(
            packed, pack_right(jnp.concatenate([integral_ref[q], empty], axis=0))
        )
    inner_ref = inner_late.get()

    def local_tile(i):
        lanes = slice(i * 128, i * 128 + 128)
        total = [inner_ref[p, :, lanes] for p in range(9)]
        for q in range(9):
            for f in range(4):
                part = local_moved[q, f * 32 : f * 32 + 20, lanes]
                for p in range(9):
                    total[p] = total[p] - minus_ref[q, p, f : f + 1, lanes] * part
        for p in range(9):
            out_ref[p, :, lanes] = total[p]

    def plus_tile(f, i):
        lanes = slice(i * 128, i * 128 + 128)
        total = [out_ref[p, :, lanes] for p in range(9)]
        for q in range(9):
            part = moved[f, q, 0:20, lanes]
            for p in range(9):
                total[p] = total[p] - plus_ref[q, p, f : f + 1, lanes] * part
        for p in range(9):
            out_ref[p, :, lanes] = total[p]

    tiles = count // 128
    tail = jnp.zeros((40, count), f32)
    evaluate = face_expand(eval_ref, pad, face_wide)
    weight = face_expand(weight_ref, pad, face_wide)
    gauss = product_full(weight, evaluate, 1, 1) * (1.0 / time_step)
    spread = lift_expand(lift_ref, pad, wide)
    spread_ref[...] = spread.T[0:192, :]
    outer = jnp.concatenate(
        [product_full(gauss, spread[f * 64 : f * 64 + 32, 0:128]) for f in range(4)], axis=0
    )
    rows = [jnp.concatenate([integral_ref[r], empty], axis=0) for r in trace_rows[0:3]]
    own_ref[...] = product_full(outer[:, 0:96], jnp.concatenate(rows, axis=0))
    extended = jnp.concatenate(
        [integral_ref[...].reshape(216, count), lower_ref[...], upper_ref[...]], axis=1
    )
    extended = jnp.concatenate(halves(extended), axis=0)
    width = extended.shape[1]
    for f in range(4):
        pick = flags(iota((width, count), 0) == neighbor_ref[f : f + 1, :]).astype(bf16)
        found = product(extended, pick)
        packed = packed_ref[f]
        turn = orientation_ref[f : f + 1, :]
        group = turn >> 2
        inner_turn = turn & 3
        for q in range(9):
            high = found[q * 24 : q * 24 + 24]
            low = found[216 + q * 24 : 216 + q * 24 + 24]
            stack = []
            for n in range(3):
                here = group == n
                high_here = jnp.where(here, high, 0.0)
                stack += [high_here, jnp.where(here, low, 0.0), high_here]
            every = product(packed, jnp.concatenate(stack + [tail], axis=0).astype(bf16))
            chosen = every[0:24]
            for a in range(1, 4):
                chosen = jnp.where(inner_turn == a, every[a * 24 : a * 24 + 24], chosen)
            moved[f, q] = chosen
            if q % 2 and q // 2 < tiles:
                if f:
                    plus_tile(f - 1, q // 2)
                else:
                    local_tile(q // 2)
    for i in range(tiles):
        plus_tile(3, i)
    out_sent.send()


def friction_kernel(
    arrived_ref,
    position_ref,
    owner_ref,
    impedance_ref,
    eval_ref,
    weight_ref,
    normal_ref,
    shear_ref,
    slip_ref,
    static_ref,
    drop_ref,
    scale_ref,
    reply_ref,
    slip_out_ref,
    traction_ref,
    states,
    pad,
    face_wide,
):
    owned_full = owner_flags(owner_ref)
    owned = owned_full.astype(bf16)
    owned_twice = jnp.concatenate([owned, owned], axis=0)
    position = position_ref[0:1, :]
    faults = slip_ref.shape[1]
    wave = jnp.zeros((32, 2 * faults), f32)
    for r in range(6):
        high, low = halves(arrived_ref[pl.ds(r, 128, stride=6), :].T)
        found = product(jnp.concatenate([high, low], axis=1), owned_twice)
        for j in range(4):
            wave = jnp.where(position == float(4 * r + j), found[j * 32 : j * 32 + 32], wave)
    pwave_minus = impedance_ref[0:1, :]
    pwave_plus = impedance_ref[1:2, :]
    swave_minus = impedance_ref[2:3, :]
    swave_plus = impedance_ref[3:4, :]
    pwave_sum = pwave_minus + pwave_plus
    swave_sum = swave_minus + swave_plus
    viscous = swave_minus * swave_plus / swave_sum
    normal_row = iota((32, faults), 0) < 10
    modal = (
        jnp.where(normal_row, pwave_plus / pwave_sum, swave_plus / swave_sum) * wave[:, 0:faults]
        + jnp.where(normal_row, pwave_minus / pwave_sum, swave_minus / swave_sum)
        * wave[:, faults : 2 * faults]
    ) * (1.0 / time_step)
    high, low = halves(face_expand(eval_ref, pad, face_wide))
    modal_high, modal_low = halves(modal)
    states[...] = product(
        jnp.concatenate([high, high, low], axis=0),
        jnp.concatenate([modal_high, modal_low, modal_high], axis=0),
        0,
        0,
    )
    normal = states[0:25, :]
    initial = (shear_ref[:, 0, :], shear_ref[:, 1, :])
    shear = (states[32:57, :] + initial[0], states[64:89, :] + initial[1])
    weakened = jnp.minimum(slip_ref[...] / scale_ref[...], 1.0)
    coefficient = static_ref[...] - drop_ref[...] * weakened
    strength = coefficient * jnp.maximum(-(normal + normal_ref[...]), 0.0)
    magnitude = jnp.sqrt(shear[0] * shear[0] + shear[1] * shear[1])
    ratio = jnp.minimum(1.0, strength / jnp.maximum(magnitude, 1.0))
    final = (shear[0] * ratio, shear[1] * ratio)
    rate_0 = (shear[0] - final[0]) / viscous
    rate_1 = (shear[1] - final[1]) / viscous
    slip_out_ref[...] = slip_ref[...] + time_step * jnp.sqrt(rate_0 * rate_0 + rate_1 * rate_1)
    traction_ref[:, 0, :] = final[0]
    traction_ref[:, 1, :] = final[1]
    states[32:57, :] = final[0] - initial[0]
    states[64:89, :] = final[1] - initial[1]
    weight_high, weight_low = halves(face_expand(weight_ref, pad, face_wide))
    high, low = halves(states[...])
    imposed = product(
        jnp.concatenate([weight_high, weight_low], axis=0), high
    )
    imposed = imposed[0:32] + imposed[32:64] + product(weight_high, low)
    high = imposed.astype(bf16).astype(f32)
    low = imposed - high
    high = jnp.concatenate([high, high], axis=1)
    low = jnp.concatenate([low, low], axis=1)
    later = position >= 12.0
    within = jnp.where(later, position - 12.0, position)
    split = jnp.concatenate(
        [jnp.where(later, 0.0, owned_full), jnp.where(later, owned_full, 0.0)], axis=0
    ).astype(bf16)
    highs = []
    lows = []
    for k in range(12):
        here = within == float(k)
        highs.append(jnp.where(here, high, 0.0).astype(bf16))
        lows.append(jnp.where(here, low, 0.0).astype(bf16))
    blocks = product(jnp.concatenate(highs + lows, axis=0), split, 1, 1)
    blocks = blocks[0:384] + blocks[384:768]
    for r in range(6):
        lane = r // 3 * 128
        row = r % 3 * 128
        reply_ref[pl.ds(r, 128, stride=6), :] = blocks[row : row + 128, lane : lane + 128].T


def final_kernel(
    request_ref,
    returned_ref,
    own_ref,
    spread_ref,
    partial_ref,
    out_ref,
    totals,
    rows,
    arrive,
    leave,
):
    arriving = [
        pltpu.make_async_copy(partial_ref.at[p], rows.at[k], arrive.at[k])
        for k, p in enumerate(trace_rows)
    ]
    leaving = [
        pltpu.make_async_copy(rows.at[k], out_ref.at[p], leave.at[k])
        for k, p in enumerate(trace_rows)
    ]
    for copy in arriving:
        copy.start()
    count = own_ref.shape[1]
    request = request_ref[...]
    turned = request.T
    element, face = slots_of(turned)
    inverse = jnp.where(turned == 0.0, 0.0, 1.0 / jnp.where(turned == 0.0, 1.0, turned))
    row = iota((32, 128), 0)
    normal_row = (row < 10) | (row == 30)
    for r in range(6):
        block = returned_ref[pl.ds(r, 128, stride=6), :].T
        highs = []
        lows = []
        for j in range(4):
            k = 4 * r + j
            plain = jnp.where(row >= 30, 1.0, block[j * 32 : j * 32 + 32])
            scale = jnp.where(normal_row, inverse[24 + k : 25 + k, :], inverse[48 + k : 49 + k, :])
            mine = jnp.concatenate([plain, plain * scale], axis=0)
            side = face[k : k + 1, :]
            high, low = halves(mine)
            here = [flags(side == f).astype(bf16) for f in range(4)]
            highs.append(jnp.concatenate([high * h for h in here], axis=0))
            lows.append(jnp.concatenate([low * h for h in here], axis=0))
        values = jnp.concatenate(
            [jnp.concatenate(highs, axis=1), jnp.concatenate(lows, axis=1)], axis=0
        )
        pick = slot_flags(element, 4 * r, 4, count)
        part = product(values, pick, 1, 1)
        part = part[0:256] + part[256:512]
        if r:
            totals[...] += part
        else:
            totals[...] = part
    row = iota((32, count), 0) < 10
    states = []
    for f in range(4):
        base = f * 64
        own = own_ref[f * 32 : f * 32 + 32, :]
        sides = totals[base + 30 : base + 31, :]
        scaled = jnp.where(row, totals[base + 62 : base + 63, :], totals[base + 63 : base + 64, :])
        states.append(totals[base : base + 32, :] - sides * own)
        states.append(totals[base + 32 : base + 64, :] - scaled * own)
    high, low = halves(jnp.concatenate(states, axis=0))
    spread_high, spread_low = halves(spread_ref[...])
    fault = product(
        jnp.concatenate([spread_high, spread_high, spread_low], axis=1),
        jnp.concatenate([high, low, high], axis=0),
    )
    for k in range(6):
        arriving[k].wait()
        rows[k] = rows[k] + fault[k * 32 : k * 32 + 20, :]
        leaving[k].start()
    for copy in leaving:
        copy.wait()


class Arriving:
    def __init__(self, copy, ref):
        self.copy = copy
        self.ref = ref

    def get(self):
        self.copy.wait()
        return self.ref


class Leaving:
    def __init__(self, copy, ref):
        self.copy = copy
        self.ref = ref

    def send(self):
        self.copy.start()


def call(
    kernel, name, outs, scratch, operands, flops, late=(), sent=(), half=(), through=((), ()), aliases=None, room=20
):
    inputs = len(operands)
    outputs = len(outs)
    own = len(scratch)

    def body(*refs):
        sources = list(refs[:inputs])
        targets = list(refs[inputs : inputs + outputs])
        spare = refs[inputs + outputs + own : -1]
        flags_ref = refs[-1]
        for index, place in enumerate(late):
            copy = pltpu.make_async_copy(sources[place], spare[index], flags_ref.at[index])
            copy.start()
            sources[place] = Arriving(copy, spare[index])
        leaving = []
        for index, place in enumerate(sent, len(late)):
            copy = pltpu.make_async_copy(spare[index], targets[place], flags_ref.at[index])
            targets[place] = Leaving(copy, spare[index])
            leaving.append(copy)
        kernel(*sources, *targets, *refs[inputs + outputs : inputs + outputs + own])
        for copy in leaving:
            copy.wait()

    far = pl.BlockSpec(memory_space=pltpu.HBM)
    return pl.pallas_call(
        body,
        name=name,
        out_shape=[
            jax.ShapeDtypeStruct(shape, bf16 if i in half else f32) for i, shape in enumerate(outs)
        ],
        in_specs=[far if i in late or i in through[0] else vmem for i in range(inputs)],
        out_specs=[far if i in sent or i in through[1] else vmem for i in range(outputs)],
        scratch_shapes=[pltpu.VMEM(shape, f32) for shape in scratch]
        + [pltpu.VMEM(operands[i].shape, operands[i].dtype) for i in late]
        + [pltpu.VMEM(outs[i], f32) for i in sent]
        + [pltpu.SemaphoreType.DMA((max(1, len(late) + len(sent)),))],
        input_output_aliases=aliases or {},
        compiler_params=pltpu.CompilerParams(vmem_limit_bytes=room * 1024 * 1024),
        cost_estimate=pl.CostEstimate(flops=flops, bytes_accessed=4_000_000, transcendentals=0),
    )(*operands)


def exchange(block):
    return lax.all_to_all(block, both, split_axis=0, concat_axis=0, tiled=True)


def per_device(
    dofs,
    star,
    stiff,
    flux_local,
    flux_neighbor,
    solver_minus,
    solver_plus,
    neighbor,
    orientation,
    copy_list,
    face_lift,
    face_eval,
    face_weight,
    side_owner,
    side_face,
    impedance,
    normal_initial,
    shear_initial,
    slip,
    static_friction,
    friction_drop,
    slip_scale,
):
    count = dofs.shape[2]
    faults = side_owner.shape[0]
    owner = jnp.transpose(side_owner)
    wanted = jnp.transpose(side_face)
    star = jnp.transpose(star, (1, 2, 0, 3))
    minus = jnp.transpose(solver_minus, (1, 2, 0, 3))
    plus = jnp.transpose(solver_plus, (1, 2, 0, 3))
    local = jnp.transpose(flux_local, (1, 0, 2))
    flux = jnp.transpose(flux_neighbor, (1, 2, 0, 3))
    lift = jnp.transpose(face_lift, (1, 0, 2))
    evaluate = jnp.transpose(face_eval)
    shear = jnp.transpose(shear_initial, (1, 0, 2))
    request, position = call(
        request_kernel,
        "request",
        [(128, 128), (8, 2 * faults)],
        [],
        [owner, wanted, impedance],
        10**8,
        late=(0, 1, 2),
        room=60,
    )
    asked = exchange(request.reshape(128, 1, 128)).reshape(128, 128)
    integral, modal, low, up = call(
        predictor_kernel,
        "predictor",
        [(9, 24, count), (256, count), (216, 128), (216, 128)],
        [(9, 32, count), (9, 96, count), (96, 128), (16, 128), (256, 256)],
        [dofs, star, stiff, lift, copy_list],
        10**10,
    )
    (payload,) = call(gather_kernel, "gather", [(768, 128)], [], [asked, modal], 10**9)
    arrived = exchange(payload.reshape(128, 1, 768)).reshape(768, 128)
    inner, packed, low, up = call(
        inner_kernel,
        "inner",
        [(9, 20, count), (4, 96, 256), (216, 128), (216, 128)],
        [(96, 128), (128, 128), (9, 96, count), (3, 96, 256)],
        [integral, dofs, star, stiff, flux, low, up],
        10**10,
        sent=(0,),
        half=(1,),
        through=((5, 6), (2, 3)),
        aliases={5: 2, 6: 3},
    )
    from_lower = from_behind(up, both, 1)
    from_upper = from_behind(low, both, -1)
    reply, new_slip, traction = call(
        friction_kernel,
        "friction",
        [(768, 128), (25, faults), (25, 2, faults)],
        [(96, faults), (16, 128), (32, 128)],
        [
            arrived,
            position,
            owner,
            impedance,
            evaluate,
            face_weight,
            normal_initial,
            shear,
            slip,
            static_friction,
            friction_drop,
            slip_scale,
        ],
        10**9,
    )
    returned = exchange(reply.reshape(128, 1, 768)).reshape(768, 128)
    partial, own, spread = call(
        neighbour_kernel,
        "neighbour",
        [(9, 20, count), (128, count), (192, 256)],
        [(128, 128), (4, 9, 24, count), (9, 128, count), (16, 128), (256, 256), (32, 128)],
        [
            inner,
            integral,
            from_lower,
            from_upper,
            neighbor,
            orientation,
            plus,
            packed,
            minus,
            local,
            lift,
            evaluate,
            face_weight,
        ],
        10**10,
        late=(0,),
        sent=(0,),
        aliases={0: 0},
    )
    far = pl.BlockSpec(memory_space=pltpu.HBM)
    new_dofs = pl.pallas_call(
        final_kernel,
        name="final",
        out_shape=jax.ShapeDtypeStruct((9, 20, count), f32),
        in_specs=[vmem, vmem, vmem, vmem, far],
        out_specs=far,
        scratch_shapes=[
            pltpu.VMEM((256, count), f32),
            pltpu.VMEM((6, 20, count), f32),
            pltpu.SemaphoreType.DMA((6,)),
            pltpu.SemaphoreType.DMA((6,)),
        ],
        input_output_aliases={4: 0},
        compiler_params=pltpu.CompilerParams(vmem_limit_bytes=20 * 1024 * 1024),
        cost_estimate=pl.CostEstimate(flops=10**9, bytes_accessed=4_000_000, transcendentals=0),
    )(asked, returned, own, spread, partial)
    return (new_dofs, new_slip, jnp.transpose(traction, (1, 0, 2)))


def solution(mesh):
    in_specs = (
        P(None, None, ("dom", "sub")),
        P(None, None, None, ("dom", "sub")),
        P(),
        P(),
        P(),
        P(None, None, None, ("dom", "sub")),
        P(None, None, None, ("dom", "sub")),
        P(None, ("dom", "sub")),
        P(None, ("dom", "sub")),
        P(None, ("dom", "sub")),
        P(),
        P(),
        P(),
        P(("dom", "sub"), None),
        P(("dom", "sub"), None),
        P(None, ("dom", "sub")),
        P(None, ("dom", "sub")),
        P(None, None, ("dom", "sub")),
        P(None, ("dom", "sub")),
        P(None, ("dom", "sub")),
        P(None, ("dom", "sub")),
        P(None, ("dom", "sub")),
    )
    out_specs = (
        P(None, None, ("dom", "sub")),
        P(None, ("dom", "sub")),
        P(None, None, ("dom", "sub")),
    )
    return jax.shard_map(
        per_device, mesh=mesh, in_specs=in_specs, out_specs=out_specs, check_vma=False
    )
```

```python
import jax
import jax.numpy as jnp
from jax import lax
from jax.experimental import pallas as pl
from jax.experimental.pallas import tpu as pltpu
from jax.sharding import Mesh
from jax.sharding import PartitionSpec as P

time_step = 0.8
trace_rows = (0, 3, 5, 6, 7, 8)
both = ("x", "z", "core", "y")
f32 = jnp.float32
bf16 = jnp.bfloat16
vmem = pl.BlockSpec(memory_space=pltpu.VMEM)


def from_behind(block, axis, distance):
    devices = range(lax.axis_size(axis))
    route = [(i - distance, i) for i in devices if i - distance in devices]
    return lax.ppermute(block, axis, route)


def iota(shape, axis):
    return lax.broadcasted_iota(jnp.int32, shape, axis)


def product(a, b, left=1, right=0):
    return lax.dot_general(a, b, (((left,), (right,)), ((), ())), preferred_element_type=f32)


def product_full(a, b, left=1, right=0):
    return lax.dot_general(
        a,
        b,
        (((left,), (right,)), ((), ())),
        precision=lax.Precision.HIGHEST,
        preferred_element_type=f32,
    )


def halves(x):
    high = x.astype(bf16)
    low = (x - high.astype(f32)).astype(bf16)
    return high, low


def flags(condition):
    return jnp.where(condition, 1.0, 0.0).astype(f32)


def pack_left(a):
    wide = a + pltpu.roll(a, 32, 1)
    wide = wide + pltpu.roll(wide, 64, 1)
    high = wide.astype(bf16).astype(f32)
    return jnp.where(iota(wide.shape, 1) < 64, high, wide - high).astype(bf16)


def pack_right(x):
    high, low = halves(x)
    return jnp.concatenate([high, low, high, low], axis=0)


def thirds(t):
    return jnp.where(t >= 10, 1, 0) + jnp.where(t >= 20, 1, 0)


def owner_flags(owner_ref):
    owner = jnp.concatenate([owner_ref[0:1, :], owner_ref[1:2, :]], axis=1)
    core = (owner >> 2) & 1
    owner = core * 64 + (owner >> 5) * 16 + (owner & 3) * 4 + ((owner >> 3) & 3)
    return flags(iota((128, owner.shape[1]), 0) == owner)


def request_kernel(owner_late, face_late, impedance_late, request_ref, position_ref):
    owned = owner_flags(owner_late.get())
    owned_half = owned.astype(bf16)
    sides = owned.shape[1]
    block = 256
    ahead = flags(iota((block, block), 0) < iota((block, block), 1)).astype(bf16)
    carry = jnp.zeros((128, 1), f32)
    positions = []
    for start in range(0, sides, block):
        part = owned[:, start : start + block]
        before = product(owned_half[:, start : start + block], ahead) + carry
        positions.append(jnp.sum(part * before, axis=0, keepdims=True))
        carry = carry + jnp.sum(part, axis=1, keepdims=True)
    position = jnp.concatenate(positions, axis=1)
    position_ref[...] = jnp.broadcast_to(position, position_ref.shape)
    face_ref = face_late.get()
    impedance_ref = impedance_late.get()
    wanted = jnp.concatenate([face_ref[0:1, :], face_ref[1:2, :]], axis=1).astype(f32) + 1.0
    zp = jnp.concatenate([impedance_ref[0:1, :], -impedance_ref[1:2, :]], axis=1)
    zs = jnp.concatenate([impedance_ref[2:3, :], -impedance_ref[3:4, :]], axis=1)
    row = iota((128, sides), 0)
    channel = jnp.where(row >= 24, 1, 0) + jnp.where(row >= 48, 1, 0)
    slot = (row - 24 * channel).astype(f32)
    value = jnp.where(row < 24, wanted, jnp.where(row < 48, zp, zs))
    value = jnp.where((slot == position) & (row < 72), value, 0.0)
    wide = product(owned_half, jnp.concatenate(halves(value), axis=0), 1, 1)
    request_ref[...] = wide[:, 0:128] + wide[:, 128:256]


def lift_expand(lift_ref, pad, wide):
    pad[...] = jnp.zeros_like(pad)
    wide[...] = jnp.zeros_like(wide)
    for face in range(4):
        pad[0:10, 0:20] = lift_ref[:, face, :]
        block = pad[...]
        for k in range(6):
            first = face * 64 + (k // 3) * 32 + (k % 3) * 10
            lane = k // 4 * 128
            moved = pltpu.roll(block, 32 * (k % 4), 1) if k % 4 else block
            wide[first : first + 10, lane : lane + 128] = moved[0:10]
    return wide[...]


def face_expand(face_ref, pad, wide):
    pad[...] = jnp.zeros_like(pad)
    wide[...] = jnp.zeros_like(wide)
    pad[0:10, 0:25] = face_ref[...]
    block = pad[...]
    for j in range(3):
        moved = pltpu.roll(block, 32 * j, 1) if j else block
        wide[j * 10 : j * 10 + 10, :] = moved[0:10]
    return wide[:, 0:96]


def pack_turns(flux_ref, packed_ref, turns):
    turns[...] = jnp.zeros_like(turns)
    lane = iota((96, 256), 1)
    lane = lane - jnp.where(lane >= 72, 72, 0) - jnp.where(lane >= 144, 72, 0)
    for f in range(4):
        wide = jnp.zeros((96, 256), f32)
        for n in range(3):
            for a in range(4):
                turns[n, a * 24 : a * 24 + 20, 0:20] = flux_ref[n * 4 + a, :, f, :]
            wide = wide + (pltpu.roll(turns[n], n * 72, 1) if n else turns[n])
        wide = wide + pltpu.roll(wide, 24, 1) + pltpu.roll(wide, 48, 1)
        high = wide.astype(bf16).astype(f32)
        packed_ref[f] = jnp.where(lane < 48, high, wide - high).astype(bf16)


def predictor_kernel(
    dofs_ref,
    star_ref,
    stiff_ref,
    lift_ref,
    copy_ref,
    integral_ref,
    modal_ref,
    low_ref,
    up_ref,
    current,
    moved,
    left,
    pad,
    wide,
):
    count = dofs_ref.shape[2]
    left[...] = jnp.zeros_like(left)
    for d in range(3):
        left[d * 32 : d * 32 + 20, 0:20] = stiff_ref[d]
    packed = pack_left(left[...])
    current[...] = jnp.zeros_like(current)
    for q in range(9):
        current[q, 0:20, :] = dofs_ref[q]
        integral_ref[q, :, :] = time_step * current[q, 0:24, :]
    factor = time_step
    for order in range(1, 4):
        factor = factor * time_step / (order + 1)
        for q in range(9):
            moved[q] = product(packed, pack_right(current[q]))

        def tile(i, carry):
            lanes = pl.ds(pl.multiple_of(i * 128, 128), 128)
            total = [jnp.zeros((24, 128), f32) for _ in range(9)]
            for q in range(9):
                for d in range(3):
                    part = moved[q, d * 32 : d * 32 + 24, lanes]
                    for p in range(9):
                        total[p] = total[p] - star_ref[q, p, d : d + 1, lanes] * part
            for p in range(9):
                current[p, 0:24, lanes] = total[p]
                integral_ref[p, :, lanes] += factor * total[p]
            return carry

        lax.fori_loop(0, count // 128, tile, 0)
    whole = jnp.concatenate(halves(integral_ref[...].reshape(216, count)), axis=0)
    wanted = jnp.concatenate([copy_ref[0:1, :], copy_ref[1:2, :]], axis=1)
    found = product(whole, flags(iota((count, 256), 0) == wanted).astype(bf16))
    found = found[0:216] + found[216:432]
    low_ref[...] = found[:, 0:128]
    up_ref[...] = found[:, 128:256]
    spread = lift_expand(lift_ref, pad, wide)[:, 0:192]
    for p in range(9):
        current[p, 0:24, :] = integral_ref[p]
    rows = jnp.concatenate([current[r] for r in trace_rows], axis=0)
    rows_high, rows_low = halves(rows)
    spread_high, spread_low = halves(spread)
    modal = (
        product(spread_high, rows_high)
        + product(spread_high, rows_low)
        + product(spread_low, rows_high)
    )
    modal_ref[...] = modal


def slots_of(request):
    wanted = (request + 0.5).astype(jnp.int32) - 1
    element = jnp.where(wanted < 0, -1, wanted & 511)
    return element, wanted >> 9


def slot_flags(element, first, many, count):
    row = iota((count, 128), 0)
    return jnp.concatenate(
        [flags(element[k : k + 1, :] == row).astype(bf16) for k in range(first, first + many)],
        axis=1,
    )


def gather_kernel(request_ref, modal_ref, out_ref):
    turned = request_ref[...].T
    element, face = slots_of(turned)
    modal = jnp.concatenate(halves(modal_ref[...]), axis=0)
    normal_row = iota((32, 128), 0) < 10
    for r in range(6):
        pick = slot_flags(element, 4 * r, 4, modal_ref.shape[1])
        found = product(modal, pick)
        found = found[0:256] + found[256:512]
        waves = []
        for j in range(4):
            k = 4 * r + j
            mine = found[:, j * 128 : j * 128 + 128]
            side = face[k : k + 1, :]
            state = mine[0:64]
            for f in range(1, 4):
                state = jnp.where(side == f, mine[f * 64 : f * 64 + 64], state)
            z = jnp.where(normal_row, turned[24 + k : 25 + k, :], turned[48 + k : 49 + k, :])
            waves.append(state[0:32] - z * state[32:64])
        out_ref[pl.ds(r, 128, stride=6), :] = jnp.concatenate(waves, axis=0).T


def inner_kernel(
    integral_ref,
    dofs_ref,
    star_ref,
    stiff_ref,
    flux_ref,
    low_ref,
    up_ref,
    out_sent,
    packed_ref,
    low_out_ref,
    up_out_ref,
    left,
    square,
    moved,
    turns,
):
    pack_turns(flux_ref, packed_ref, turns)
    out_ref = out_sent.ref
    left[...] = jnp.zeros_like(left)
    square[...] = jnp.zeros_like(square)
    for d in range(3):
        square[0:20, 0:20] = stiff_ref[d]
        left[d * 32 : d * 32 + 32, :] = square[...].T[0:32, :]
    packed = pack_left(left[...])
    count = integral_ref.shape[2]
    empty = jnp.zeros((8, count), f32)
    for q in range(9):
        moved[q] = product(
            packed, pack_right(jnp.concatenate([integral_ref[q], empty], axis=0))
        )

    def tile(i, carry):
        lanes = pl.ds(pl.multiple_of(i * 128, 128), 128)
        total = [dofs_ref[p, :, lanes] for p in range(9)]
        for q in range(9):
            for d in range(3):
                part = moved[q, d * 32 : d * 32 + 20, lanes]
                for p in range(9):
                    total[p] = total[p] + star_ref[q, p, d : d + 1, lanes] * part
        for p in range(9):
            out_ref[p, :, lanes] = total[p]
        return carry

    lax.fori_loop(0, count // 128, tile, 0, unroll=True)
    out_sent.send()


def neighbour_kernel(
    inner_late,
    integral_ref,
    lower_ref,
    upper_ref,
    neighbor_ref,
    orientation_ref,
    plus_ref,
    packed_ref,
    minus_ref,
    local_ref,
    lift_ref,
    eval_ref,
    weight_ref,
    out_sent,
    own_ref,
    spread_ref,
    left,
    moved,
    local_moved,
    pad,
    wide,
    face_wide,
):
    count = integral_ref.shape[2]
    out_ref = out_sent.ref
    empty = jnp.zeros((8, count), f32)
    left[...] = jnp.zeros_like(left)
    for f in range(4):
        left[f * 32 : f * 32 + 20, 0:20] = local_ref[:, f, :]
    packed = pack_left(left[...])
    for q in range(9):
        local_moved[q] = product(
            packed, pack_right(jnp.concatenate([integral_ref[q], empty], axis=0))
        )
    inner_ref = inner_late.get()

    def local_tile(i):
        lanes = slice(i * 128, i * 128 + 128)
        total = [inner_ref[p, :, lanes] for p in range(9)]
        for q in range(9):
            for f in range(4):
                part = local_moved[q, f * 32 : f * 32 + 20, lanes]
                for p in range(9):
                    total[p] = total[p] - minus_ref[q, p, f : f + 1, lanes] * part
        for p in range(9):
            out_ref[p, :, lanes] = total[p]

    def plus_tile(f, i):
        lanes = slice(i * 128, i * 128 + 128)
        total = [out_ref[p, :, lanes] for p in range(9)]
        for q in range(9):
            part = moved[f, q, 0:20, lanes]
            for p in range(9):
                total[p] = total[p] - plus_ref[q, p, f : f + 1, lanes] * part
        for p in range(9):
            out_ref[p, :, lanes] = total[p]

    tiles = count // 128
    tail = jnp.zeros((40, count), f32)
    evaluate = face_expand(eval_ref, pad, face_wide)
    weight = face_expand(weight_ref, pad, face_wide)
    gauss = product_full(weight, evaluate, 1, 1) * (1.0 / time_step)
    spread = lift_expand(lift_ref, pad, wide)
    spread_ref[...] = spread.T[0:192, :]
    outer = jnp.concatenate(
        [product_full(gauss, spread[f * 64 : f * 64 + 32, 0:128]) for f in range(4)], axis=0
    )
    rows = [jnp.concatenate([integral_ref[r], empty], axis=0) for r in trace_rows[0:3]]
    own_ref[...] = product_full(outer[:, 0:96], jnp.concatenate(rows, axis=0))
    extended = jnp.concatenate(
        [integral_ref[...].reshape(216, count), lower_ref[...], upper_ref[...]], axis=1
    )
    extended = jnp.concatenate(halves(extended), axis=0)
    width = extended.shape[1]
    for f in range(4):
        pick = flags(iota((width, count), 0) == neighbor_ref[f : f + 1, :]).astype(bf16)
        found = product(extended, pick)
        packed = packed_ref[f]
        turn = orientation_ref[f : f + 1, :]
        group = turn >> 2
        inner_turn = turn & 3
        for q in range(9):
            high = found[q * 24 : q * 24 + 24]
            low = found[216 + q * 24 : 216 + q * 24 + 24]
            stack = []
            for n in range(3):
                here = group == n
                high_here = jnp.where(here, high, 0.0)
                stack += [high_here, jnp.where(here, low, 0.0), high_here]
            every = product(packed, jnp.concatenate(stack + [tail], axis=0).astype(bf16))
            chosen = every[0:24]
            for a in range(1, 4):
                chosen = jnp.where(inner_turn == a, every[a * 24 : a * 24 + 24], chosen)
            moved[f, q] = chosen
            if q % 2 and q // 2 < tiles:
                if f:
                    plus_tile(f - 1, q // 2)
                else:
                    local_tile(q // 2)
    for i in range(tiles):
        plus_tile(3, i)
    out_sent.send()


def friction_kernel(
    arrived_ref,
    position_ref,
    owner_ref,
    impedance_ref,
    eval_ref,
    weight_ref,
    normal_ref,
    shear_ref,
    slip_ref,
    static_ref,
    drop_ref,
    scale_ref,
    reply_ref,
    slip_out_ref,
    traction_ref,
    states,
    pad,
    face_wide,
):
    owned_full = owner_flags(owner_ref)
    owned = owned_full.astype(bf16)
    owned_twice = jnp.concatenate([owned, owned], axis=0)
    position = position_ref[0:1, :]
    faults = slip_ref.shape[1]
    wave = jnp.zeros((32, 2 * faults), f32)
    for r in range(6):
        high, low = halves(arrived_ref[pl.ds(r, 128, stride=6), :].T)
        found = product(jnp.concatenate([high, low], axis=1), owned_twice)
        for j in range(4):
            wave = jnp.where(position == float(4 * r + j), found[j * 32 : j * 32 + 32], wave)
    pwave_minus = impedance_ref[0:1, :]
    pwave_plus = impedance_ref[1:2, :]
    swave_minus = impedance_ref[2:3, :]
    swave_plus = impedance_ref[3:4, :]
    pwave_sum = pwave_minus + pwave_plus
    swave_sum = swave_minus + swave_plus
    viscous = swave_minus * swave_plus / swave_sum
    normal_row = iota((32, faults), 0) < 10
    modal = (
        jnp.where(normal_row, pwave_plus / pwave_sum, swave_plus / swave_sum) * wave[:, 0:faults]
        + jnp.where(normal_row, pwave_minus / pwave_sum, swave_minus / swave_sum)
        * wave[:, faults : 2 * faults]
    ) * (1.0 / time_step)
    high, low = halves(face_expand(eval_ref, pad, face_wide))
    modal_high, modal_low = halves(modal)
    states[...] = product(
        jnp.concatenate([high, high, low], axis=0),
        jnp.concatenate([modal_high, modal_low, modal_high], axis=0),
        0,
        0,
    )
    normal = states[0:25, :]
    initial = (shear_ref[:, 0, :], shear_ref[:, 1, :])
    shear = (states[32:57, :] + initial[0], states[64:89, :] + initial[1])
    weakened = jnp.minimum(slip_ref[...] / scale_ref[...], 1.0)
    coefficient = static_ref[...] - drop_ref[...] * weakened
    strength = coefficient * jnp.maximum(-(normal + normal_ref[...]), 0.0)
    magnitude = jnp.sqrt(shear[0] * shear[0] + shear[1] * shear[1])
    ratio = jnp.minimum(1.0, strength / jnp.maximum(magnitude, 1.0))
    final = (shear[0] * ratio, shear[1] * ratio)
    rate_0 = (shear[0] - final[0]) / viscous
    rate_1 = (shear[1] - final[1]) / viscous
    slip_out_ref[...] = slip_ref[...] + time_step * jnp.sqrt(rate_0 * rate_0 + rate_1 * rate_1)
    traction_ref[:, 0, :] = final[0]
    traction_ref[:, 1, :] = final[1]
    states[32:57, :] = final[0] - initial[0]
    states[64:89, :] = final[1] - initial[1]
    weight_high, weight_low = halves(face_expand(weight_ref, pad, face_wide))
    high, low = halves(states[...])
    imposed = product(
        jnp.concatenate([weight_high, weight_low], axis=0), high
    )
    imposed = imposed[0:32] + imposed[32:64] + product(weight_high, low)
    high = imposed.astype(bf16).astype(f32)
    low = imposed - high
    high = jnp.concatenate([high, high], axis=1)
    low = jnp.concatenate([low, low], axis=1)
    later = position >= 12.0
    within = jnp.where(later, position - 12.0, position)
    split = jnp.concatenate(
        [jnp.where(later, 0.0, owned_full), jnp.where(later, owned_full, 0.0)], axis=0
    ).astype(bf16)
    highs = []
    lows = []
    for k in range(12):
        here = within == float(k)
        highs.append(jnp.where(here, high, 0.0).astype(bf16))
        lows.append(jnp.where(here, low, 0.0).astype(bf16))
    blocks = product(jnp.concatenate(highs + lows, axis=0), split, 1, 1)
    blocks = blocks[0:384] + blocks[384:768]
    for r in range(6):
        lane = r // 3 * 128
        row = r % 3 * 128
        reply_ref[pl.ds(r, 128, stride=6), :] = blocks[row : row + 128, lane : lane + 128].T


def final_kernel(
    request_ref,
    returned_ref,
    own_ref,
    spread_ref,
    partial_ref,
    out_ref,
    totals,
    rows,
    arrive,
    leave,
):
    arriving = [
        pltpu.make_async_copy(partial_ref.at[p], rows.at[k], arrive.at[k])
        for k, p in enumerate(trace_rows)
    ]
    leaving = [
        pltpu.make_async_copy(rows.at[k], out_ref.at[p], leave.at[k])
        for k, p in enumerate(trace_rows)
    ]
    for copy in arriving:
        copy.start()
    count = own_ref.shape[1]
    request = request_ref[...]
    turned = request.T
    element, face = slots_of(turned)
    inverse = jnp.where(turned == 0.0, 0.0, 1.0 / jnp.where(turned == 0.0, 1.0, turned))
    row = iota((32, 128), 0)
    normal_row = (row < 10) | (row == 30)
    for r in range(6):
        block = returned_ref[pl.ds(r, 128, stride=6), :].T
        highs = []
        lows = []
        for j in range(4):
            k = 4 * r + j
            plain = jnp.where(row >= 30, 1.0, block[j * 32 : j * 32 + 32])
            scale = jnp.where(normal_row, inverse[24 + k : 25 + k, :], inverse[48 + k : 49 + k, :])
            mine = jnp.concatenate([plain, plain * scale], axis=0)
            side = face[k : k + 1, :]
            high, low = halves(mine)
            here = [flags(side == f).astype(bf16) for f in range(4)]
            highs.append(jnp.concatenate([high * h for h in here], axis=0))
            lows.append(jnp.concatenate([low * h for h in here], axis=0))
        values = jnp.concatenate(
            [jnp.concatenate(highs, axis=1), jnp.concatenate(lows, axis=1)], axis=0
        )
        pick = slot_flags(element, 4 * r, 4, count)
        part = product(values, pick, 1, 1)
        part = part[0:256] + part[256:512]
        if r:
            totals[...] += part
        else:
            totals[...] = part
    row = iota((32, count), 0) < 10
    states = []
    for f in range(4):
        base = f * 64
        own = own_ref[f * 32 : f * 32 + 32, :]
        sides = totals[base + 30 : base + 31, :]
        scaled = jnp.where(row, totals[base + 62 : base + 63, :], totals[base + 63 : base + 64, :])
        states.append(totals[base : base + 32, :] - sides * own)
        states.append(totals[base + 32 : base + 64, :] - scaled * own)
    high, low = halves(jnp.concatenate(states, axis=0))
    spread_high, spread_low = halves(spread_ref[...])
    fault = product(
        jnp.concatenate([spread_high, spread_high, spread_low], axis=1),
        jnp.concatenate([high, low, high], axis=0),
    )
    for k in range(6):
        arriving[k].wait()
        rows[k] = rows[k] + fault[k * 32 : k * 32 + 20, :]
        leaving[k].start()
    for copy in leaving:
        copy.wait()


class Arriving:
    def __init__(self, copy, ref):
        self.copy = copy
        self.ref = ref

    def get(self):
        self.copy.wait()
        return self.ref


class Leaving:
    def __init__(self, copy, ref):
        self.copy = copy
        self.ref = ref

    def send(self):
        self.copy.start()


def call(
    kernel, name, outs, scratch, operands, flops, late=(), sent=(), half=(), through=((), ()), aliases=None, room=20
):
    inputs = len(operands)
    outputs = len(outs)
    own = len(scratch)

    def body(*refs):
        sources = list(refs[:inputs])
        targets = list(refs[inputs : inputs + outputs])
        spare = refs[inputs + outputs + own : -1]
        flags_ref = refs[-1]
        for index, place in enumerate(late):
            copy = pltpu.make_async_copy(sources[place], spare[index], flags_ref.at[index])
            copy.start()
            sources[place] = Arriving(copy, spare[index])
        leaving = []
        for index, place in enumerate(sent, len(late)):
            copy = pltpu.make_async_copy(spare[index], targets[place], flags_ref.at[index])
            targets[place] = Leaving(copy, spare[index])
            leaving.append(copy)
        kernel(*sources, *targets, *refs[inputs + outputs : inputs + outputs + own])
        for copy in leaving:
            copy.wait()

    far = pl.BlockSpec(memory_space=pltpu.HBM)
    return pl.pallas_call(
        body,
        name=name,
        out_shape=[
            jax.ShapeDtypeStruct(shape, bf16 if i in half else f32) for i, shape in enumerate(outs)
        ],
        in_specs=[far if i in late or i in through[0] else vmem for i in range(inputs)],
        out_specs=[far if i in sent or i in through[1] else vmem for i in range(outputs)],
        scratch_shapes=[pltpu.VMEM(shape, f32) for shape in scratch]
        + [pltpu.VMEM(operands[i].shape, operands[i].dtype) for i in late]
        + [pltpu.VMEM(outs[i], f32) for i in sent]
        + [pltpu.SemaphoreType.DMA((max(1, len(late) + len(sent)),))],
        input_output_aliases=aliases or {},
        compiler_params=pltpu.CompilerParams(vmem_limit_bytes=room * 1024 * 1024),
        cost_estimate=pl.CostEstimate(flops=flops, bytes_accessed=4_000_000, transcendentals=0),
    )(*operands)


def exchange(block):
    return lax.all_to_all(block, ("core", "x", "y", "z"), split_axis=0, concat_axis=0, tiled=True)


def per_device(
    dofs,
    star,
    stiff,
    flux_local,
    flux_neighbor,
    solver_minus,
    solver_plus,
    neighbor,
    orientation,
    copy_list,
    face_lift,
    face_eval,
    face_weight,
    side_owner,
    side_face,
    impedance,
    normal_initial,
    shear_initial,
    slip,
    static_friction,
    friction_drop,
    slip_scale,
):
    count = dofs.shape[2]
    faults = side_owner.shape[0]
    owner = jnp.transpose(side_owner)
    wanted = jnp.transpose(side_face)
    star = jnp.transpose(star, (1, 2, 0, 3))
    minus = jnp.transpose(solver_minus, (1, 2, 0, 3))
    plus = jnp.transpose(solver_plus, (1, 2, 0, 3))
    local = jnp.transpose(flux_local, (1, 0, 2))
    flux = jnp.transpose(flux_neighbor, (1, 2, 0, 3))
    lift = jnp.transpose(face_lift, (1, 0, 2))
    evaluate = jnp.transpose(face_eval)
    shear = jnp.transpose(shear_initial, (1, 0, 2))
    request, position = call(
        request_kernel,
        "request",
        [(128, 128), (8, 2 * faults)],
        [],
        [owner, wanted, impedance],
        10**8,
        late=(0, 1, 2),
        room=60,
    )
    asked = exchange(request.reshape(128, 1, 128)).reshape(128, 128)
    integral, modal, low, up = call(
        predictor_kernel,
        "predictor",
        [(9, 24, count), (256, count), (216, 128), (216, 128)],
        [(9, 32, count), (9, 96, count), (96, 128), (16, 128), (256, 256)],
        [dofs, star, stiff, lift, copy_list],
        10**10,
    )
    (payload,) = call(gather_kernel, "gather", [(768, 128)], [], [asked, modal], 10**9)
    arrived = exchange(payload.reshape(128, 1, 768)).reshape(768, 128)
    inner, packed, low, up = call(
        inner_kernel,
        "inner",
        [(9, 20, count), (4, 96, 256), (216, 128), (216, 128)],
        [(96, 128), (128, 128), (9, 96, count), (3, 96, 256)],
        [integral, dofs, star, stiff, flux, low, up],
        10**10,
        sent=(0,),
        half=(1,),
        through=((5, 6), (2, 3)),
        aliases={5: 2, 6: 3},
    )
    from_lower = from_behind(up, both, 1)
    from_upper = from_behind(low, both, -1)
    reply, new_slip, traction = call(
        friction_kernel,
        "friction",
        [(768, 128), (25, faults), (25, 2, faults)],
        [(96, faults), (16, 128), (32, 128)],
        [
            arrived,
            position,
            owner,
            impedance,
            evaluate,
            face_weight,
            normal_initial,
            shear,
            slip,
            static_friction,
            friction_drop,
            slip_scale,
        ],
        10**9,
    )
    returned = exchange(reply.reshape(128, 1, 768)).reshape(768, 128)
    partial, own, spread = call(
        neighbour_kernel,
        "neighbour",
        [(9, 20, count), (128, count), (192, 256)],
        [(128, 128), (4, 9, 24, count), (9, 128, count), (16, 128), (256, 256), (32, 128)],
        [
            inner,
            integral,
            from_lower,
            from_upper,
            neighbor,
            orientation,
            plus,
            packed,
            minus,
            local,
            lift,
            evaluate,
            face_weight,
        ],
        10**10,
        late=(0,),
        sent=(0,),
        aliases={0: 0},
    )
    far = pl.BlockSpec(memory_space=pltpu.HBM)
    new_dofs = pl.pallas_call(
        final_kernel,
        name="final",
        out_shape=jax.ShapeDtypeStruct((9, 20, count), f32),
        in_specs=[vmem, vmem, vmem, vmem, far],
        out_specs=far,
        scratch_shapes=[
            pltpu.VMEM((256, count), f32),
            pltpu.VMEM((6, 20, count), f32),
            pltpu.SemaphoreType.DMA((6,)),
            pltpu.SemaphoreType.DMA((6,)),
        ],
        input_output_aliases={4: 0},
        compiler_params=pltpu.CompilerParams(vmem_limit_bytes=20 * 1024 * 1024),
        cost_estimate=pl.CostEstimate(flops=10**9, bytes_accessed=4_000_000, transcendentals=0),
    )(asked, returned, own, spread, partial)
    return (new_dofs, new_slip, jnp.transpose(traction, (1, 0, 2)))


def solution(mesh):
    fine = Mesh(mesh.devices.reshape(4, 4, 2, 4), both)
    in_specs = (
        P(None, None, both),
        P(None, None, None, both),
        P(),
        P(),
        P(),
        P(None, None, None, both),
        P(None, None, None, both),
        P(None, both),
        P(None, both),
        P(None, both),
        P(),
        P(),
        P(),
        P(both, None),
        P(both, None),
        P(None, both),
        P(None, both),
        P(None, None, both),
        P(None, both),
        P(None, both),
        P(None, both),
        P(None, both),
    )
    out_specs = (
        P(None, None, both),
        P(None, both),
        P(None, None, both),
    )
    return jax.shard_map(
        per_device, mesh=fine, in_specs=in_specs, out_specs=out_specs, check_vma=False
    )
```
